256 devices in a mesh: cond: 4 (over z_hi), space: 64 (over z_lo, y, x, core).
Axes of the slice: x: 4, y: 4, z: 8 (z_hi: 4, z_lo: 2; z = z_hi * 2 + z_lo), core: 2. Of those that a mesh axis runs over, the one named last changes fastest.
Arguments:
- objective_grad: float32 [8, 5, 256, 8, 128], P('cond', None, 'space'), may hold values from -18 to 18
- shape_derivative: float32 [8, 5, 256, 8, 128], P('cond', None, 'space'), may hold values from -6 to 6
- flux_jacobian: float32 [8, 3, 5, 5], P('cond'), may hold values from -2 to 2
- sensor: float32 [8, 256, 8, 128], P('cond', 'space'), may hold values from 0.1 to 1
- pseudo_shift: float32 [8], P('cond'), may hold values from 1 to 3
- objective_weight: float32 [8], P('cond'), may hold values from 0.3 to 3
- agglomeration: int32 [256, 8, 128], P('space'), may hold values from 0 to 127, as said below
- coarse_links: int32 [6, 8192], P(None, 'space'), may hold values from 0 to 8191, as said below
Outputs:
- adjoint: float32 [8, 5, 256, 8, 128], P('cond', None, 'space')
- mesh_sensitivity: float32 [256, 8, 128], P('space', 'cond')
The draws below stay inside these ranges and needn't reach their ends.
Inputs may be any that keep to these rules, and one draw needn't show every extreme that they name: `agglomeration`: each value names the cells of one box of 2 x 4 x 4 cells of the block (boxes aligned to the block), numbered in a random order within each block of 4 cells along the first dimension. `coarse_links`: the entries of a coarse cell are its six face neighbours on the grid of boxes; where a neighbour would lie outside the grid, the cell names itself. Every entry lies in the cell's own block or in a block beside it along the first dimension.
All inputs are finite; a program needn't handle non-finite values.
Results may differ from the reference program's by a relative error of at most 0.0001.
Values sent between devices are 32-bit elements; how exact they have to be, the bound alone decides.
A program may use at most 64 MiB of HBM per device.

```python
import math
import jax
import jax.numpy as jnp
from jax import lax

CX = 4
NY = 8
NZ = 128
AGG = 32
LINKS = 6
CYCLES = 2
SWEEPS = 3
CSWEEPS = 4
COND = 8
NX = 256
COARSE_DEV = 128
NC = 8192


def block_labels(key):
    key = jax.random.fold_in(key, 11)
    blocks = NX // CX

    def one_block(position):
        return jax.random.permutation(jax.random.fold_in(key, position), COARSE_DEV).astype(jnp.int32)
    return jax.lax.map(one_block, jnp.arange(blocks, dtype=jnp.int32))


def draw_agglomeration(key, part):
    labels = block_labels(key)
    boxes_y = NY // 4
    boxes_z = NZ // 4
    xs = jnp.arange(NX, dtype=jnp.int32)
    ys = jnp.arange(NY, dtype=jnp.int32)
    zs = jnp.arange(NZ, dtype=jnp.int32)
    block = xs // CX
    box = (xs % CX // 2)[:, None, None] * (boxes_y * boxes_z) + (ys // 4)[None, :, None] * boxes_z + (zs // 4)[None, None, :]
    block_full = jnp.broadcast_to(block[:, None, None], box.shape)
    return labels[block_full, box].astype(jnp.int32)


def draw_coarse_links(key, part):
    labels = block_labels(key)
    half = CX // 2
    grid_x = NX // 2
    grid_y = NY // 4
    grid_z = NZ // 4
    gx = jnp.broadcast_to(jnp.arange(grid_x, dtype=jnp.int32)[:, None, None], (grid_x, grid_y, grid_z))
    gy = jnp.broadcast_to(jnp.arange(grid_y, dtype=jnp.int32)[None, :, None], (grid_x, grid_y, grid_z))
    gz = jnp.broadcast_to(jnp.arange(grid_z, dtype=jnp.int32)[None, None, :], (grid_x, grid_y, grid_z))

    def ident(px, py, pz):
        block = px // half
        box = (px % half * grid_y + py) * grid_z + pz
        return labels[block, box] + block * COARSE_DEV
    own = ident(gx, gy, gz)
    linked = []
    for dx, dy, dz in ((-1, 0, 0), (1, 0, 0), (0, -1, 0), (0, 1, 0), (0, 0, -1), (0, 0, 1)):
        nx = gx + dx
        ny = gy + dy
        nz = gz + dz
        valid = (nx >= 0) & (nx < grid_x) & (ny >= 0) & (ny < grid_y) & (nz >= 0) & (nz < grid_z)
        other = ident(jnp.clip(nx, 0, grid_x - 1), jnp.clip(ny, 0, grid_y - 1), jnp.clip(nz, 0, grid_z - 1))
        linked.append(jnp.where(valid, other, own).reshape(-1))
    stacked = jnp.stack(linked, axis=0).astype(jnp.int32)
    result = jnp.zeros((LINKS, NC), jnp.int32)
    return result.at[:, own.reshape(-1)].set(stacked).astype(jnp.int32)


def levels(key, shape, split, least, top_value):
    gain, own = 1.0, jax.random.fold_in(key, 6)
    for axis_at, parts in split:
        draws = jnp.exp(jax.random.uniform(jax.random.fold_in(own, axis_at), (parts,), jnp.float32, least / len(split), top_value / len(split)))
        gain = gain * jnp.repeat(draws, shape[axis_at] // parts).reshape([-1 if axis == axis_at else 1 for axis in range(len(shape))])
    return gain


def normal_values(own_key, dims, deviation, bound, shards=(), held_as=jnp.bfloat16):
    loudness = levels(own_key, dims, shards, -0.22, 0.18) if shards else 1.0
    entries = jax.random.normal(own_key, dims, jnp.float32) * deviation * loudness
    return jnp.minimum(jnp.maximum(entries, -bound), bound).astype(held_as)


def setup_inputs(seed: int = 0) -> dict:
    splits = jax.random.split(jax.random.key(seed), 9)
    objective_grad = normal_values(splits[0], (COND, 5, NX, NY, NZ), 3.0, 18.0, ((0, 4), (2, 64)), jnp.float32)
    shape_derivative = normal_values(splits[1], (COND, 5, NX, NY, NZ), 1.0, 6.0, ((0, 4), (2, 64)), jnp.float32)
    flux_jacobian = normal_values(splits[2], (COND, 3, 5, 5), 10 ** -0.5, 2.0, ((0, 4),), jnp.float32)
    sensor = jnp.clip(jnp.exp(math.log(1.0) - 2.3025851 * jax.random.uniform(splits[3], (COND, NX, NY, NZ), jnp.float32) ** levels(splits[3], (COND, NX, NY, NZ), ((0, 4), (1, 64)), -0.2, 0.2)), 0.1, 1.0)
    pseudo_shift = jnp.clip(1.0 + 2.0 * jax.random.uniform(splits[4], (COND,), jnp.float32) ** levels(splits[4], (COND,), ((0, 4),), -0.2, 0.2), 1.0, 3.0)
    objective_weight = jnp.clip(jnp.exp(math.log(3.0) - 2.3025851 * jax.random.uniform(splits[5], (COND,), jnp.float32) ** levels(splits[5], (COND,), ((0, 4),), -0.2, 0.2)), 0.3, 3.0)
    agglomeration = draw_agglomeration(jax.random.fold_in(splits[8], 71), 0)
    coarse_links = draw_coarse_links(jax.random.fold_in(splits[8], 71), 0)
    return {"objective_grad": objective_grad, "shape_derivative": shape_derivative, "flux_jacobian": flux_jacobian, "sensor": sensor, "pseudo_shift": pseudo_shift, "objective_weight": objective_weight, "agglomeration": agglomeration, "coarse_links": coarse_links}


EPS_FOURTH = 1.0 / 32.0
RELAX = 0.7


def window(values, leading, margin, direction, displace):
    selection = []
    for i in range(values.ndim):
        if i < leading:
            selection.append(slice(None))
        else:
            length = values.shape[i] - 2 * margin
            offset = margin + (displace if i - leading == direction else 0)
            selection.append(slice(offset, offset + length))
    return values[tuple(selection)]


def coefficients(sensor_pad, shift):
    center = window(sensor_pad, 1, 1, 0, 0)
    face_plus = []
    face_minus = []
    summed = jnp.zeros_like(center)
    for d in range(3):
        face_plus.append((center + window(sensor_pad, 1, 1, d, 1)) * 0.25)
        face_minus.append((center + window(sensor_pad, 1, 1, d, -1)) * 0.25)
        summed = summed + (face_plus[d] + face_minus[d])
    diagonal_fine = shift[:, None, None, None] + summed + 18.0 * EPS_FOURTH
    return face_plus, face_minus, diagonal_fine


def operate(field_x, face_plus, face_minus, jacobians, shift):
    extended = jnp.pad(field_x, ((0, 0), (0, 0), (0, 0), (2, 2), (2, 2)))
    center = window(extended, 2, 2, 0, 0)
    result = shift[:, None, None, None, None] * center
    for d in range(3):
        plus_one = window(extended, 2, 2, d, 1)
        minus_one = window(extended, 2, 2, d, -1)
        plus_two = window(extended, 2, 2, d, 2)
        minus_two = window(extended, 2, 2, d, -2)
        central = 0.5 * jnp.einsum("cuv,cuxyz->cvxyz", jacobians[:, d], minus_one - plus_one, precision=lax.Precision.HIGHEST)
        second = face_plus[d][:, None] * (plus_one - center) - face_minus[d][:, None] * (center - minus_one)
        fourth = EPS_FOURTH * (plus_two + minus_two - 4.0 * (plus_one + minus_one) + 6.0 * center)
        result = result + (central - second + fourth)
    return result


def coarse_sweep(current, lookup, coarse_res, links, diagonal_coarse, coupling):
    neighbour_sum = jnp.sum(lookup[:, :, links], axis=2)
    return current + (coarse_res - diagonal_coarse * current + coupling * neighbour_sum) / diagonal_coarse


def reference(objective_grad, shape_derivative, flux_jacobian, sensor, pseudo_shift, objective_weight, agglomeration, coarse_links):
    block_base = (jnp.arange(NX, dtype=jnp.int32) // CX) * COARSE_DEV
    global_ids = (block_base[:, None, None] + agglomeration).reshape(-1).astype(jnp.int32)
    coupling = AGG / 4.0

    def solve_condition(items):
        target, derivative, jacobians, sensor_c, shift, weight = items
        target = target[None]
        jacobians = jacobians[None]
        shift = shift[None]
        sensor_pad = jnp.pad(sensor_c[None], ((0, 0), (1, 1), (1, 1), (1, 1)))
        face_plus, face_minus, diagonal_fine = coefficients(sensor_pad, shift)

        def residual_of(adjoint):
            padded = jnp.pad(adjoint, ((0, 0), (0, 0), (2, 2), (0, 0), (0, 0)))
            return target - operate(padded, face_plus, face_minus, jacobians, shift)

        diagonal_coarse = (shift * AGG + LINKS * AGG / 4.0)[:, None, None]
        adjoint = jnp.zeros_like(target)
        for cycle in range(CYCLES):
            for sweep in range(SWEEPS):
                adjoint = adjoint + RELAX * residual_of(adjoint) / diagonal_fine[:, None]
            fine_res = residual_of(adjoint)
            flattened = fine_res.reshape(5, -1)
            coarse_res = jax.ops.segment_sum(flattened.T, global_ids, num_segments=NC).T[None]
            correction = coarse_res / diagonal_coarse
            for step in range(CSWEEPS - 1):
                correction = coarse_sweep(correction, correction, coarse_res, coarse_links, diagonal_coarse, coupling)
            adjoint = adjoint + correction[:, :, global_ids].reshape(adjoint.shape)
        contribution = weight * jnp.sum(adjoint[0] * derivative, axis=0)
        return adjoint[0], contribution

    adjoints, contributions = lax.map(solve_condition, (objective_grad, shape_derivative, flux_jacobian, sensor, pseudo_shift, objective_weight))
    return adjoints, jnp.sum(contributions, axis=0)
```

```python
import functools

import jax
import jax.numpy as jnp
from jax import lax
from jax.experimental import pallas as pl
from jax.experimental.pallas import tpu as pltpu
from jax.sharding import PartitionSpec as P

RELAX = 0.7
EPS = 1.0 / 32.0
F32 = jnp.float32
STEP = 2


def sublanes(shape):
    return lax.broadcasted_iota(jnp.int32, shape, len(shape) - 2)


def lanes(shape):
    return lax.broadcasted_iota(jnp.int32, shape, len(shape) - 1)


def up(a, n):
    return pltpu.roll(a, 8 - n, a.ndim - 2)


def down(a, n):
    return pltpu.roll(a, n, a.ndim - 2)


def ahead(a, n):
    return pltpu.roll(a, 128 - n, a.ndim - 1)


def behind(a, n):
    return pltpu.roll(a, n, a.ndim - 1)


def pack(v):
    s, z = sublanes(v[0].shape), lanes(v[0].shape)
    even, low = s % 2 == 0, s % 4 < 2
    zeven, zlow = z % 2 == 0, z % 4 < 2

    def pair(a, b):
        return jnp.where(even, a, b) + jnp.where(even, up(a, 1), down(b, 1))

    def quad(a, b):
        return jnp.where(low, a, b) + jnp.where(low, up(a, 2), down(b, 2))

    four = quad(pair(v[0], v[1]), pair(v[2], v[3]))
    last = pair(v[4], v[4])
    last = quad(last, last)
    both = jnp.where(zeven, four, last) + jnp.where(zeven, ahead(four, 1), behind(last, 1))
    return both + jnp.where(zlow, ahead(both, 2), behind(both, 2))


def unpack(c):
    s, z = sublanes(c.shape), lanes(c.shape)
    even, low, zeven = s % 2 == 0, s % 4 < 2, z % 2 == 0
    four = jnp.where(zeven, c, behind(c, 1))
    last = jnp.where(zeven, ahead(c, 1), c)
    p02 = jnp.where(even, four, down(four, 1))
    p13 = jnp.where(even, up(four, 1), four)
    return (
        jnp.where(low, p02, down(p02, 2)),
        jnp.where(low, p13, down(p13, 2)),
        jnp.where(low, up(p02, 2), p02),
        jnp.where(low, up(p13, 2), p13),
        last,
    )


def coarse_solve(res, first, last_box, inverse):
    beta = 8.0 * inverse
    scaled = res * inverse
    c = scaled
    for sweep in range(1, 4):
        own = c[1:-1]
        at = first + sweep + lax.broadcasted_iota(jnp.int32, own.shape, 0)
        z = lanes(own.shape)
        total = jnp.where(at == 0, own, c[:-2]) + jnp.where(at == last_box, own, c[2:])
        total = total + (own + up(own, 4))
        total = total + jnp.where(z < 4, own, behind(own, 4)) + jnp.where(z >= 124, own, ahead(own, 4))
        c = scaled[sweep:-sweep] + beta * total
    return c


def off_diagonal(field, at, n, jac, cpx, cyz):
    shape = (n, 8, 128)
    s, z = sublanes(shape), lanes(shape)
    center = [field[u, pl.ds(at, n)] for u in range(5)]
    cx_plus, cx_minus = cpx[pl.ds(at - 1, n)], cpx[pl.ds(at - 2, n)]
    cy_plus, cy_minus, cz_plus, cz_minus = (cyz[i, pl.ds(at - 2, n)] for i in range(4))
    out = []
    diffs = []
    for u in range(5):
        a = center[u]
        plus, minus = field[u, pl.ds(at + 1, n)], field[u, pl.ds(at - 1, n)]
        far = field[u, pl.ds(at + 2, n)] + field[u, pl.ds(at - 2, n)]
        near = cx_plus * plus + cx_minus * minus
        dx = plus - minus
        plus, minus = up(a, 1), down(a, 1)
        far = far + jnp.where(s < 6, up(a, 2), 0.0) + jnp.where(s >= 2, down(a, 2), 0.0)
        near = near + (cy_plus * plus + cy_minus * minus)
        dy = jnp.where(s < 7, plus, 0.0) - jnp.where(s >= 1, minus, 0.0)
        plus, minus = ahead(a, 1), behind(a, 1)
        far = far + jnp.where(z < 126, ahead(a, 2), 0.0) + jnp.where(z >= 2, behind(a, 2), 0.0)
        near = near + (cz_plus * plus + cz_minus * minus)
        dz = jnp.where(z < 127, plus, 0.0) - jnp.where(z >= 1, minus, 0.0)
        out.append(near - EPS * far)
        diffs.append((dx, dy, dz))
    for v in range(5):
        for d in range(3):
            for u in range(5):
                out[v] = out[v] + jac[d * 25 + u * 5 + v] * diffs[u][d]
    return center, out


def kernel(
    n_cond, n_space, target_in, shape_in, jac_in, sensor_in, shift_in, weight_in, adjoint_out, sens_out,
    g, sen, shp, cpx, cyz, w, diag, jac, b0, b1, halo, rs, rp1, rp2, cs, rc, local_sem, send_sem, recv_sem,
):
    space, cond = lax.axis_index("space"), lax.axis_index("cond")
    chip, core = space // 2, space % 2
    chips = n_space // 2
    has_left, has_right = chip > 0, chip < chips - 1
    has_left2, has_right2 = chip > 1, chip < chips - 2
    rows = 8 // n_cond

    barrier = pltpu.get_barrier_semaphore()
    peers = [(2 * chip + 1 - core, cond, None)]
    for near, there in ((-1, has_left), (1, has_right)):
        peers += [(2 * (chip + near) + j, cond, there) for j in range(2)]
    for far, there in ((-2, has_left2), (2, has_right2)):
        peers.append((2 * (chip + far) + core, cond, there))
    ring = [(2 * chip + (core + j) % 2, lax.rem(cond + dz, n_cond)) for dz in range(n_cond) for j in range(2)]
    peers += [(s, c, None) for s, c in ring[2:]]
    for s, c, there in peers:
        def greet(s=s, c=c):
            pl.semaphore_signal(barrier, inc=1, device_id={"space": s, "cond": c})
        greet() if there is None else pl.when(there)(greet)

    count = iter(range(1000))
    sends = []

    def remote(src, dst, recv, s, c=cond):
        return pltpu.make_async_remote_copy(
            src_ref=src, dst_ref=dst, send_sem=send_sem.at[next(count)], recv_sem=recv_sem.at[recv],
            device_id={"space": s, "cond": c},
        )

    mine = [
        pltpu.make_async_copy(target_in.at[core], g.at[:, pl.ds(6 + 4 * core, 4)], local_sem.at[0]),
        pltpu.make_async_copy(sensor_in.at[core], sen.at[pl.ds(7 + 4 * core, 4)], local_sem.at[1]),
        pltpu.make_async_copy(shape_in.at[core], shp.at[:, pl.ds(4 * core, 4)], local_sem.at[2]),
    ]
    for copy in mine:
        copy.start()

    @pl.when(jnp.logical_not(has_left))
    def _():
        g[:, 0:6] = jnp.zeros((5, 6, 8, 128), F32)
        sen[0:7] = jnp.zeros((7, 8, 128), F32)
        halo[:, 0:6] = jnp.zeros((5, 6, 8, 128), F32)
        rp1[3:7] = jnp.zeros((4, 8, 128), F32)
        rp2[0:3] = jnp.zeros((3, 8, 128), F32)

    @pl.when(jnp.logical_not(has_right))
    def _():
        g[:, 14:20] = jnp.zeros((5, 6, 8, 128), F32)
        sen[15:22] = jnp.zeros((7, 8, 128), F32)
        halo[:, 6:12] = jnp.zeros((5, 6, 8, 128), F32)
        rp1[11:15] = jnp.zeros((4, 8, 128), F32)
        rp2[7:10] = jnp.zeros((3, 8, 128), F32)

    @pl.when(jnp.logical_not(has_left2))
    def _():
        rp1[0:3] = jnp.zeros((3, 8, 128), F32)

    @pl.when(jnp.logical_not(has_right2))
    def _():
        rp1[15:18] = jnp.zeros((3, 8, 128), F32)

    for d in range(3):
        for u in range(5):
            for v in range(5):
                jac[d * 25 + u * 5 + v] = jnp.full((8, 128), 0.5 * jac_in[core, d, u, v], F32)
    shift = jnp.full((8, 128), shift_in[core], F32)
    inverse = 1.0 / (shift * 32.0 + 48.0)

    n_peers = 1 + 2 * (n_cond - 1)
    pl.semaphore_wait(
        barrier,
        n_peers + 2 * has_left.astype(jnp.int32) + 2 * has_right.astype(jnp.int32)
        + has_left2.astype(jnp.int32) + has_right2.astype(jnp.int32),
    )

    def to_right(k, j):
        low, size, at = ((2, 2, 0), (0, 4, 2))[k]
        s_low, s_size, s_at = ((1, 3, 0), (0, 4, 3))[k]
        there = 2 * (chip + 1) + j
        return [
            remote(sensor_in.at[j, pl.ds(s_low, s_size)], sen.at[pl.ds(s_at, s_size)], 3 + 2 * k, there),
            remote(target_in.at[j, :, pl.ds(low, size)], g.at[:, pl.ds(at, size)], 4 + 2 * k, there),
        ]

    def to_left(k, j):
        size, at = ((4, 14), (2, 18))[k]
        s_size, s_at = ((4, 15), (3, 19))[k]
        there = 2 * (chip - 1) + j
        return [
            remote(sensor_in.at[j, pl.ds(0, s_size)], sen.at[pl.ds(s_at, s_size)], 7 + 2 * k, there),
            remote(target_in.at[j, :, pl.ds(0, size)], g.at[:, pl.ds(at, size)], 8 + 2 * k, there),
        ]

    first_round = []
    for k in range(2):
        for j in range(2):
            for make, there in ((to_right, has_right), (to_left, has_left)):
                first_round.append((make(k, j), jnp.logical_and(there, core == k)))
    for copies, there in first_round:
        @pl.when(there)
        def _(copies=copies):
            for copy in copies:
                copy.start()
    other = 1 - core
    sibling = 2 * chip + other
    swap = [
        remote(sensor_in.at[other], sen.at[pl.ds(7 + 4 * core, 4)], 0, sibling),
        remote(target_in.at[other], g.at[:, pl.ds(6 + 4 * core, 4)], 1, sibling),
        remote(shape_in.at[other], shp.at[:, pl.ds(4 * core, 4)], 2, sibling),
    ]
    for copy in swap:
        copy.start()

    for copy in mine:
        copy.wait()
    for copy in swap:
        copy.wait_recv()
    for k in range(2):
        for make, there in ((to_right, has_left), (to_left, has_right)):
            copies = make(k, 0)

            @pl.when(there)
            def _(copies=copies):
                for copy in copies:
                    copy.wait_recv()

    s, z = sublanes((1, 8, 128)), lanes((1, 8, 128))

    def coefficients(i, carry):
        near = sen[pl.ds(i + 1, 1)]
        x_plus, x_minus = (near + sen[pl.ds(i + 2, 1)]) * 0.25, (near + sen[pl.ds(i, 1)]) * 0.25
        y_plus = (near + jnp.where(s < 7, up(near, 1), 0.0)) * 0.25
        y_minus = (near + jnp.where(s >= 1, down(near, 1), 0.0)) * 0.25
        z_plus = (near + jnp.where(z < 127, ahead(near, 1), 0.0)) * 0.25
        z_minus = (near + jnp.where(z >= 1, behind(near, 1), 0.0)) * 0.25
        total = shift[None] + ((x_plus + x_minus) + (y_plus + y_minus) + (z_plus + z_minus)) + 18.0 * EPS
        cpx[pl.ds(i + 1, 1)] = x_plus + 4.0 * EPS
        cyz[0, pl.ds(i, 1)] = jnp.where(s < 7, y_plus + 4.0 * EPS, 0.0)
        cyz[1, pl.ds(i, 1)] = jnp.where(s >= 1, y_minus + 4.0 * EPS, 0.0)
        cyz[2, pl.ds(i, 1)] = jnp.where(z < 127, z_plus + 4.0 * EPS, 0.0)
        cyz[3, pl.ds(i, 1)] = jnp.where(z >= 1, z_minus + 4.0 * EPS, 0.0)
        inside = jnp.logical_and(jnp.logical_or(has_left, i >= 6), jnp.logical_or(has_right, i < 14))
        weight = jnp.where(inside, RELAX / total, 0.0)
        diag[pl.ds(i, 1)] = total
        w[pl.ds(i, 1)] = weight
        for v in range(5):
            b0[v, pl.ds(i + 2, 1)] = weight * g[v, pl.ds(i, 1)]
        return carry

    cpx[0:1] = (sen[0:1] + sen[1:2]) * 0.25 + 4.0 * EPS
    lax.fori_loop(0, 20, coefficients, 0)

    def sweep(src, dst, low, high):
        def body(i, carry):
            at = low + i * STEP
            center, out = off_diagonal(src, at, STEP, jac, cpx, cyz)
            weight = w[pl.ds(at - 2, STEP)]
            for v in range(5):
                dst[v, pl.ds(at, STEP)] = (1.0 - RELAX) * center[v] + weight * (g[v, pl.ds(at - 2, STEP)] + out[v])
            return carry

        lax.fori_loop(0, (high - low) // STEP, body, 0)

    def restrict(src):
        def body(i, carry):
            at = 8 + i * 2
            center, out = off_diagonal(src, at, 2, jac, cpx, cyz)
            d = diag[pl.ds(at - 2, 2)]
            for v in range(5):
                r = g[v, pl.ds(at - 2, 2)] + out[v] - d * center[v]
                rs[v, pl.ds(i, 1)] = r[0:1] + r[1:2]
            return carry

        lax.fori_loop(0, 4, body, 0)
        return pack([rs[v] for v in range(5)])

    right, left = space + 2, space - 2

    def start(copies):
        for copy, there in copies:
            pl.when(there)(copy.start)

    def arrive(copies, theres):
        for (copy, _), there in zip(copies, theres):
            pl.when(there)(copy.wait_recv)

    def sent(copies):
        for copy, there in copies:
            pl.when(there)(copy.wait_send)

    sweep(b0, b1, 4, 20)
    sweep(b1, b0, 6, 18)
    halos = [
        (remote(b0.at[:, pl.ds(8, 6)], halo.at[:, pl.ds(0, 6)], 11, right), has_right),
        (remote(b0.at[:, pl.ds(10, 6)], halo.at[:, pl.ds(6, 6)], 12, left), has_left),
    ]
    start(halos)
    rp1[7:11] = restrict(b0)
    boxes = [
        (remote(rp1.at[pl.ds(8, 3)], rp1.at[pl.ds(0, 3)], 13, space + 4), has_right2),
        (remote(rp1.at[pl.ds(7, 3)], rp1.at[pl.ds(15, 3)], 14, space - 4), has_left2),
        (remote(rp1.at[pl.ds(7, 4)], rp1.at[pl.ds(3, 4)], 15, right), has_right),
        (remote(rp1.at[pl.ds(7, 4)], rp1.at[pl.ds(11, 4)], 16, left), has_left),
    ]
    start(boxes)
    arrive(halos, (has_left, has_right))
    arrive(boxes, (has_left2, has_right2, has_left, has_right))
    last_box = 4 * chips - 1
    c = coarse_solve(rp1[...], 4 * chip - 7, last_box, inverse[None])
    at = 4 * chip - 4 + lax.broadcasted_iota(jnp.int32, c.shape, 0)
    c = jnp.where(jnp.logical_and(at >= 0, at <= last_box), c, 0.0)
    rs1 = unpack(c)
    for v in range(5):
        for i in range(12):
            add = rs1[v][i]
            for j in (2 * i, 2 * i + 1):
                old = halo[v, j] if j < 6 else b0[v, j] if j < 18 else halo[v, j - 12]
                b1[v, j] = old + add
    sent(halos)

    sweep(b1, b0, 2, 22)
    sweep(b0, b1, 4, 20)
    sweep(b1, b0, 6, 18)
    rp2[3:7] = restrict(b0)
    boxes2 = [
        (remote(rp2.at[pl.ds(4, 3)], rp2.at[pl.ds(0, 3)], 17, right), has_right),
        (remote(rp2.at[pl.ds(3, 3)], rp2.at[pl.ds(7, 3)], 18, left), has_left),
    ]
    start(boxes2)
    arrive(boxes2, (has_left, has_right))
    c = coarse_solve(rp2[...], 4 * chip - 3, last_box, inverse[None])
    fixes = unpack(c)
    weight = jnp.full((8, 128), weight_in[core], F32)
    parts = []
    for i in range(8):
        total = None
        for v in range(5):
            new = b0[v, 8 + i] + fixes[v][i // 2]
            b1[v, 8 + i] = new
            term = new * shp[v, i]
            total = term if total is None else total + term
        parts.append(weight * total)

    s2 = sublanes((8, 128))
    for j in range(2):
        for c_to in range(n_cond):
            gathered = None
            for i in range(4):
                turn = (rows * i - rows * c_to) % 8
                moved = parts[4 * j + i] if turn == 0 else down(parts[4 * j + i], turn)
                gathered = moved if gathered is None else jnp.where(s2 >= rows * i, moved, gathered)
            cs[j * n_cond + c_to] = gathered
    me = 2 * cond + core
    shares = []
    for i, (s_to, c_to) in enumerate(ring[1:]):
        shares.append(remote(cs.at[lax.rem(s_to, 2) * n_cond + c_to], rc.at[me], 19 + i, s_to, c_to))
    for copy in reversed(shares):
        copy.start()
    back = remote(b1.at[:, pl.ds(8 + 4 * other, 4)], adjoint_out.at[core], 26, sibling)
    back.start()
    keep = pltpu.make_async_copy(b1.at[:, pl.ds(8 + 4 * core, 4)], adjoint_out.at[core], local_sem.at[0])
    keep.start()
    rc[me] = cs[core * n_cond + cond]
    for copy in shares:
        copy.wait_recv()
    total = rc[0]
    for i in range(1, 2 * n_cond):
        total = total + rc[i]
    for i in range(4):
        sens_out[i] = total[rows * i : rows * (i + 1)]
    keep.wait()
    back.wait()
    for copy in shares:
        copy.wait_send()
    for copy in swap:
        copy.wait_send()
    for copies, there in first_round:
        @pl.when(there)
        def _(copies=copies):
            for copy in copies:
                copy.wait_send()
    sent(boxes)
    sent(boxes2)


def solution(mesh):
    n_cond, n_space = mesh.shape["cond"], mesh.shape["space"]
    rows = 8 // n_cond

    def local(target, shape, jac, sensor, shift, weight, agglomeration, links):
        vmem = lambda *shape: pltpu.VMEM((*shape, 8, 128), F32)
        hbm = pl.BlockSpec(memory_space=pl.ANY)
        smem = pl.BlockSpec(memory_space=pltpu.SMEM)
        return pl.pallas_call(
            functools.partial(kernel, n_cond, n_space),
            out_shape=(
                jax.ShapeDtypeStruct(target.shape, F32),
                jax.ShapeDtypeStruct((4, rows, 128), F32),
            ),
            in_specs=[hbm, hbm, smem, hbm, smem, smem],
            out_specs=(hbm, pl.BlockSpec(memory_space=pltpu.VMEM)),
            scratch_shapes=[
                vmem(5, 20), vmem(22), vmem(5, 8),
                vmem(21), vmem(4, 20), vmem(20), vmem(20), vmem(75),
                vmem(5, 24), vmem(5, 24), vmem(5, 12), vmem(5, 4),
                vmem(18), vmem(10), vmem(2 * n_cond), vmem(2 * n_cond),
                pltpu.SemaphoreType.DMA((3,)),
                pltpu.SemaphoreType.DMA((64,)),
                pltpu.SemaphoreType.DMA((27,)),
            ],
            compiler_params=pltpu.CompilerParams(
                collective_id=0, has_side_effects=True, vmem_limit_bytes=48 * 2**20
            ),
        )(target, shape, jac, sensor, shift, weight)

    in_specs = (
        P("cond", None, "space", None, None),
        P("cond", None, "space", None, None),
        P("cond", None, None, None),
        P("cond", "space", None, None),
        P("cond"),
        P("cond"),
        P("space", None, None),
        P(None, "space"),
    )
    out_specs = (P("cond", None, "space", None, None), P("space", "cond", None))
    return jax.shard_map(local, mesh=mesh, in_specs=in_specs, out_specs=out_specs, check_vma=False)
```

```python
import functools

import jax
import jax.numpy as jnp
from jax import lax
from jax.experimental import pallas as pl
from jax.experimental.pallas import tpu as pltpu
from jax.sharding import PartitionSpec as P

RELAX = 0.7
EPS = 1.0 / 32.0
F32 = jnp.float32


def sublanes(shape):
    return lax.broadcasted_iota(jnp.int32, shape, len(shape) - 2)


def lanes(shape):
    return lax.broadcasted_iota(jnp.int32, shape, len(shape) - 1)


def up(a, n):
    return pltpu.roll(a, 8 - n, a.ndim - 2)


def down(a, n):
    return pltpu.roll(a, n, a.ndim - 2)


def ahead(a, n):
    return pltpu.roll(a, 128 - n, a.ndim - 1)


def behind(a, n):
    return pltpu.roll(a, n, a.ndim - 1)


def pack(v):
    s, z = sublanes(v[0].shape), lanes(v[0].shape)
    even, low = s % 2 == 0, s % 4 < 2
    zeven, zlow = z % 2 == 0, z % 4 < 2

    def pair(a, b):
        return jnp.where(even, a, b) + jnp.where(even, up(a, 1), down(b, 1))

    def quad(a, b):
        return jnp.where(low, a, b) + jnp.where(low, up(a, 2), down(b, 2))

    four = quad(pair(v[0], v[1]), pair(v[2], v[3]))
    last = pair(v[4], v[4])
    last = quad(last, last)
    both = jnp.where(zeven, four, last) + jnp.where(zeven, ahead(four, 1), behind(last, 1))
    return both + jnp.where(zlow, ahead(both, 2), behind(both, 2))


def unpack(c):
    s, z = sublanes(c.shape), lanes(c.shape)
    even, low, zeven = s % 2 == 0, s % 4 < 2, z % 2 == 0
    four = jnp.where(zeven, c, behind(c, 1))
    last = jnp.where(zeven, ahead(c, 1), c)
    p02 = jnp.where(even, four, down(four, 1))
    p13 = jnp.where(even, up(four, 1), four)
    return (
        jnp.where(low, p02, down(p02, 2)),
        jnp.where(low, p13, down(p13, 2)),
        jnp.where(low, up(p02, 2), p02),
        jnp.where(low, up(p13, 2), p13),
        last,
    )


def coarse_solve(res, first, last_box, inverse):
    beta = 8.0 * inverse
    scaled = res * inverse
    c = scaled
    for sweep in range(1, 4):
        own = c[1:-1]
        at = first + sweep + lax.broadcasted_iota(jnp.int32, own.shape, 0)
        z = lanes(own.shape)
        total = jnp.where(at == 0, own, c[:-2]) + jnp.where(at == last_box, own, c[2:])
        total = total + (own + up(own, 4))
        total = total + jnp.where(z < 4, own, behind(own, 4)) + jnp.where(z >= 124, own, ahead(own, 4))
        c = scaled[sweep:-sweep] + beta * total
    return c


def off_diagonal(field, at, n, jac, cpx, cyz):
    s, z = sublanes((1, 8, 128)), lanes((1, 8, 128))
    y_not_last, y_not_first = jnp.where(s < 7, 1.0, 0.0), jnp.where(s >= 1, 1.0, 0.0)
    z_not_last, z_not_first = jnp.where(z < 127, 1.0, 0.0), jnp.where(z >= 1, 1.0, 0.0)
    y_far_up, y_far_down = jnp.where(s < 6, -EPS, 0.0), jnp.where(s >= 2, -EPS, 0.0)
    z_far_up, z_far_down = jnp.where(z < 126, -EPS, 0.0), jnp.where(z >= 2, -EPS, 0.0)
    cx = cpx[pl.ds(at - 2, n + 1)]
    cy_plus, cy_minus, cz_plus, cz_minus = (cyz[i, pl.ds(at - 2, n)] for i in range(4))
    center, out = [], [None] * 5

    def add(v, term):
        out[v] = term if out[v] is None else out[v] + term

    for u in range(5):
        block = field[u, pl.ds(at - 2, n + 4)]
        a, plus, minus = block[2:-2], block[3:-1], block[1:-3]
        center.append(a)
        total = cx[1:] * plus
        total = total + cx[:-1] * minus
        total = total - EPS * (block[4:] + block[:-4])
        dx = plus - minus
        plus, minus = up(a, 1), down(a, 1)
        total = total + cy_plus * plus
        total = total + cy_minus * minus
        total = total + y_far_up * up(a, 2)
        total = total + y_far_down * down(a, 2)
        dy = y_not_last * plus - y_not_first * minus
        plus, minus = ahead(a, 1), behind(a, 1)
        total = total + cz_plus * plus
        total = total + cz_minus * minus
        total = total + z_far_up * ahead(a, 2)
        total = total + z_far_down * behind(a, 2)
        dz = z_not_last * plus - z_not_first * minus
        add(u, total)
        for d, diff in enumerate((dx, dy, dz)):
            for v in range(5):
                add(v, jac[d * 25 + u * 5 + v] * diff)
    return center, out


def kernel(
    n_cond, n_space, target_in, shape_in, jac_hbm, sensor_in, shift_hbm, weight_hbm, adjoint_out, sens_out,
    jac_in, shift_in, weight_in, g, sen, shp, cpx, cyz, w, diag, jac, b0, b1, b2, halo, rs, rp1, rp2, cs, rc, local_sem, send_sem, recv_sem,
):
    space, cond = lax.axis_index("space"), lax.axis_index("cond")
    chip, core = space // 2, space % 2
    chips = n_space // 2
    has_left, has_right = chip > 0, chip < chips - 1
    has_left2, has_right2 = chip > 1, chip < chips - 2
    rows = 8 // n_cond

    barrier = pltpu.get_barrier_semaphore()
    peers = [(2 * chip + 1 - core, cond, None)]
    for near, there in ((-1, has_left), (1, has_right)):
        peers += [(2 * (chip + near) + j, cond, there) for j in range(2)]
    for far, there in ((-2, has_left2), (2, has_right2)):
        peers.append((2 * (chip + far) + core, cond, there))
    ring = [(2 * chip + (core + j) % 2, lax.rem(cond + dz, n_cond)) for dz in range(n_cond) for j in range(2)]
    peers += [(s, c, None) for s, c in ring[2:]]
    for s, c, there in peers:
        def greet(s=s, c=c):
            pl.semaphore_signal(barrier, inc=1, device_id={"space": s, "cond": c})
        greet() if there is None else pl.when(there)(greet)

    count = iter(range(1000))
    sends = []

    def remote(src, dst, recv, s, c=cond):
        return pltpu.make_async_remote_copy(
            src_ref=src, dst_ref=dst, send_sem=send_sem.at[next(count)], recv_sem=recv_sem.at[recv],
            device_id={"space": s, "cond": c},
        )

    mine = [
        pltpu.make_async_copy(sensor_in.at[core], sen.at[pl.ds(7 + 4 * core, 4)], local_sem.at[0]),
        pltpu.make_async_copy(target_in.at[core], g.at[:, pl.ds(6 + 4 * core, 4)], local_sem.at[1]),
        pltpu.make_async_copy(shape_in.at[core], shp.at[:, pl.ds(4 * core, 4)], local_sem.at[2]),
    ]
    small = [
        pltpu.make_async_copy(jac_hbm, jac_in, local_sem.at[3]),
        pltpu.make_async_copy(shift_hbm, shift_in, local_sem.at[4]),
        pltpu.make_async_copy(weight_hbm, weight_in, local_sem.at[5]),
    ]
    for copy in small + mine:
        copy.start()

    @pl.when(jnp.logical_not(has_left))
    def _():
        g[:, 0:6] = jnp.zeros((5, 6, 8, 128), F32)
        sen[0:7] = jnp.zeros((7, 8, 128), F32)
        halo[:, 0:6] = jnp.zeros((5, 6, 8, 128), F32)
        rp1[3:7] = jnp.zeros((4, 8, 128), F32)
        rp2[0:3] = jnp.zeros((3, 8, 128), F32)

    @pl.when(jnp.logical_not(has_right))
    def _():
        g[:, 14:20] = jnp.zeros((5, 6, 8, 128), F32)
        sen[15:22] = jnp.zeros((7, 8, 128), F32)
        halo[:, 6:12] = jnp.zeros((5, 6, 8, 128), F32)
        rp1[11:15] = jnp.zeros((4, 8, 128), F32)
        rp2[7:10] = jnp.zeros((3, 8, 128), F32)

    @pl.when(jnp.logical_not(has_left2))
    def _():
        rp1[0:3] = jnp.zeros((3, 8, 128), F32)

    @pl.when(jnp.logical_not(has_right2))
    def _():
        rp1[15:18] = jnp.zeros((3, 8, 128), F32)

    for copy in small:
        copy.wait()
    for d in range(3):
        for u in range(5):
            for v in range(5):
                jac[d * 25 + u * 5 + v] = jnp.full((8, 128), 0.5 * jac_in[d, u, core, v], F32)
    shift = jnp.full((8, 128), shift_in[core], F32)
    inverse = 1.0 / (shift * 32.0 + 48.0)

    n_peers = 1 + 2 * (n_cond - 1)
    pl.semaphore_wait(
        barrier,
        n_peers + 2 * has_left.astype(jnp.int32) + 2 * has_right.astype(jnp.int32)
        + has_left2.astype(jnp.int32) + has_right2.astype(jnp.int32),
    )

    def to_right(k, j):
        low, size, at = ((2, 2, 0), (0, 4, 2))[k]
        s_low, s_size, s_at = ((1, 3, 0), (0, 4, 3))[k]
        there = 2 * (chip + 1) + j
        return [
            remote(sensor_in.at[j, pl.ds(s_low, s_size)], sen.at[pl.ds(s_at, s_size)], 3 + 2 * k, there),
            remote(target_in.at[j, :, pl.ds(low, size)], g.at[:, pl.ds(at, size)], 4 + 2 * k, there),
        ]

    def to_left(k, j):
        size, at = ((4, 14), (2, 18))[k]
        s_size, s_at = ((4, 15), (3, 19))[k]
        there = 2 * (chip - 1) + j
        return [
            remote(sensor_in.at[j, pl.ds(0, s_size)], sen.at[pl.ds(s_at, s_size)], 7 + 2 * k, there),
            remote(target_in.at[j, :, pl.ds(0, size)], g.at[:, pl.ds(at, size)], 8 + 2 * k, there),
        ]

    first_round = []
    for k in range(2):
        for make, there in ((to_right, has_right), (to_left, has_left)):
            pairs = [make(k, j) for j in range(2)]
            first_round.append(([c[0] for c in pairs] + [c[1] for c in pairs], jnp.logical_and(there, core == k)))
    other = 1 - core
    sibling = 2 * chip + other
    swap = [
        remote(sensor_in.at[other], sen.at[pl.ds(7 + 4 * core, 4)], 0, sibling),
        remote(target_in.at[other], g.at[:, pl.ds(6 + 4 * core, 4)], 1, sibling),
        remote(shape_in.at[other], shp.at[:, pl.ds(4 * core, 4)], 2, sibling),
    ]
    for copies, there in first_round:
        @pl.when(there)
        def _(copies=copies):
            for copy in copies:
                copy.start()
    for copy in swap:
        copy.start()

    awaited = [(make(k, 0), there) for k in range(2) for make, there in ((to_right, has_left), (to_left, has_right))]

    def arrive_first(i):
        mine[i].wait()
        swap[i].wait_recv()
        for copies, there in awaited:
            pl.when(there)(copies[i].wait_recv)

    arrive_first(0)

    s, z = sublanes((1, 8, 128)), lanes((1, 8, 128))

    def coefficients(k, carry):
        i = 4 * k
        block = sen[pl.ds(i, 6)]
        near = block[1:5]
        x_plus, x_minus = (near + block[2:]) * 0.25, (near + block[:4]) * 0.25
        y_plus = (near + jnp.where(s < 7, up(near, 1), 0.0)) * 0.25
        y_minus = (near + jnp.where(s >= 1, down(near, 1), 0.0)) * 0.25
        z_plus = (near + jnp.where(z < 127, ahead(near, 1), 0.0)) * 0.25
        z_minus = (near + jnp.where(z >= 1, behind(near, 1), 0.0)) * 0.25
        total = shift[None] + ((x_plus + x_minus) + (y_plus + y_minus) + (z_plus + z_minus)) + 18.0 * EPS
        cpx[pl.ds(i + 1, 4)] = x_plus + 4.0 * EPS
        cyz[0, pl.ds(i, 4)] = jnp.where(s < 7, y_plus + 4.0 * EPS, 0.0)
        cyz[1, pl.ds(i, 4)] = jnp.where(s >= 1, y_minus + 4.0 * EPS, 0.0)
        cyz[2, pl.ds(i, 4)] = jnp.where(z < 127, z_plus + 4.0 * EPS, 0.0)
        cyz[3, pl.ds(i, 4)] = jnp.where(z >= 1, z_minus + 4.0 * EPS, 0.0)
        at = i + lax.broadcasted_iota(jnp.int32, total.shape, 0)
        inside = jnp.logical_and(at >= low_layer, at < high_layer)
        diag[pl.ds(i, 4)] = total
        w[pl.ds(i, 4)] = jnp.where(inside, RELAX / total, 0.0)
        return carry

    low_layer, high_layer = jnp.where(has_left, 0, 6), jnp.where(has_right, 20, 14)
    cpx[0:1] = (sen[0:1] + sen[1:2]) * 0.25 + 4.0 * EPS
    lax.fori_loop(0, 5, coefficients, 0)
    arrive_first(1)

    def begin(k, carry):
        i = 4 * k
        weight = w[pl.ds(i, 4)]
        for v in range(5):
            b0[v, pl.ds(i + 2, 4)] = weight * g[v, pl.ds(i, 4)]
        return carry

    lax.fori_loop(0, 5, begin, 0)

    def sweep(src, dst, low, n, times, stride=None):
        def body(i, carry):
            at = low + i * (stride or n)
            center, out = off_diagonal(src, at, n, jac, cpx, cyz)
            weight = w[pl.ds(at - 2, n)]
            for v in range(5):
                dst[v, pl.ds(at, n)] = (1.0 - RELAX) * center[v] + weight * (g[v, pl.ds(at - 2, n)] + out[v])
            return carry

        lax.fori_loop(0, times, body, 0)

    def restrict(src):
        def body(i, carry):
            at = 8 + i * 4
            center, out = off_diagonal(src, at, 4, jac, cpx, cyz)
            d = diag[pl.ds(at - 2, 4)]
            for v in range(5):
                r = g[v, pl.ds(at - 2, 4)] + out[v] - d * center[v]
                rs[v, pl.ds(2 * i, 1)] = r[0:1] + r[1:2]
                rs[v, pl.ds(2 * i + 1, 1)] = r[2:3] + r[3:4]
            return carry

        lax.fori_loop(0, 2, body, 0)
        return pack([rs[v] for v in range(5)])

    right, left = space + 2, space - 2

    def start(copies):
        for copy, there in copies:
            pl.when(there)(copy.start)

    def arrive(copies, theres):
        for (copy, _), there in zip(copies, theres):
            pl.when(there)(copy.wait_recv)

    def sent(copies):
        for copy, there in copies:
            pl.when(there)(copy.wait_send)

    sweep(b0, b1, 4, 4, 4)
    sweep(b1, b0, 6, 4, 3)
    near_halos = [
        (remote(b0.at[:, pl.ds(12, 2)], halo.at[:, pl.ds(4, 2)], 11, right), has_right),
        (remote(b0.at[:, pl.ds(10, 2)], halo.at[:, pl.ds(6, 2)], 12, left), has_left),
    ]
    far_halos = [
        (remote(b0.at[:, pl.ds(8, 4)], halo.at[:, pl.ds(0, 4)], 19, right), has_right),
        (remote(b0.at[:, pl.ds(12, 4)], halo.at[:, pl.ds(8, 4)], 20, left), has_left),
    ]
    start(near_halos)
    rp1[7:11] = restrict(b0)
    boxes = [
        (remote(rp1.at[pl.ds(8, 3)], rp1.at[pl.ds(0, 3)], 13, space + 4), has_right2),
        (remote(rp1.at[pl.ds(7, 3)], rp1.at[pl.ds(15, 3)], 14, space - 4), has_left2),
        (remote(rp1.at[pl.ds(7, 4)], rp1.at[pl.ds(3, 4)], 15, right), has_right),
        (remote(rp1.at[pl.ds(7, 4)], rp1.at[pl.ds(11, 4)], 16, left), has_left),
    ]
    start(boxes)
    start(far_halos)
    arrive(boxes, (has_left2, has_right2, has_left, has_right))
    last_box = 4 * chips - 1
    c = coarse_solve(rp1[...], 4 * chip - 7, last_box, inverse[None])
    at = 4 * chip - 4 + lax.broadcasted_iota(jnp.int32, c.shape, 0)
    fixes = unpack(jnp.where(jnp.logical_and(at >= 0, at <= last_box), c, 0.0))

    def correct(old, low, high):
        for v in range(5):
            for i in range(low, high):
                b1[v, i] = old(v, i) + fixes[v][i // 2]

    correct(lambda v, i: b0[v, i], 6, 18)
    sweep(b1, b2, 8, 4, 2)
    arrive(near_halos + far_halos, (has_left, has_right) * 2)
    correct(lambda v, i: halo[v, i], 0, 6)
    correct(lambda v, i: halo[v, i - 12], 18, 24)
    sweep(b1, b2, 2, 6, 2, 14)
    sweep(b2, b1, 4, 4, 4)
    sweep(b1, b2, 6, 4, 3)
    rp2[3:7] = restrict(b2)
    boxes2 = [
        (remote(rp2.at[pl.ds(4, 3)], rp2.at[pl.ds(0, 3)], 17, right), has_right),
        (remote(rp2.at[pl.ds(3, 3)], rp2.at[pl.ds(7, 3)], 18, left), has_left),
    ]
    start(boxes2)
    arrive(boxes2, (has_left, has_right))
    c = coarse_solve(rp2[...], 4 * chip - 3, last_box, inverse[None])
    fixes = unpack(c)
    weight = jnp.full((8, 128), weight_in[core], F32)
    mine[2].wait()
    swap[2].wait_recv()
    parts = []
    for i in range(8):
        total = None
        for v in range(5):
            new = b2[v, 8 + i] + fixes[v][i // 2]
            b1[v, 8 + i] = new
            term = new * shp[v, i]
            total = term if total is None else total + term
        parts.append(weight * total)

    s2 = sublanes((8, 128))
    for j in range(2):
        for c_to in range(n_cond):
            gathered = None
            for i in range(4):
                turn = (rows * i - rows * c_to) % 8
                moved = parts[4 * j + i] if turn == 0 else down(parts[4 * j + i], turn)
                gathered = moved if gathered is None else jnp.where(s2 >= rows * i, moved, gathered)
            cs[j * n_cond + c_to] = gathered
    me = 2 * cond + core
    shares = []
    for i, (s_to, c_to) in enumerate(ring[1:]):
        shares.append(remote(cs.at[lax.rem(s_to, 2) * n_cond + c_to], rc.at[me], 21 + i, s_to, c_to))
    for copy in reversed(shares):
        copy.start()
    back = remote(b1.at[:, pl.ds(8 + 4 * other, 4)], adjoint_out.at[core], 28, sibling)
    back.start()
    keep = pltpu.make_async_copy(b1.at[:, pl.ds(8 + 4 * core, 4)], adjoint_out.at[core], local_sem.at[0])
    keep.start()
    rc[me] = cs[core * n_cond + cond]
    for copy in shares:
        copy.wait_recv()
    total = rc[0]
    for i in range(1, 2 * n_cond):
        total = total + rc[i]
    for i in range(4):
        sens_out[i] = total[rows * i : rows * (i + 1)]
    keep.wait()
    back.wait()
    for copy in shares:
        copy.wait_send()
    for copy in swap:
        copy.wait_send()
    for copies, there in first_round:
        @pl.when(there)
        def _(copies=copies):
            for copy in copies:
                copy.wait_send()
    sent(near_halos + far_halos + boxes + boxes2)


def solution(mesh):
    n_cond, n_space = mesh.shape["cond"], mesh.shape["space"]
    rows = 8 // n_cond

    def local(target, shape, jac, sensor, shift, weight, agglomeration, links):
        vmem = lambda *shape: pltpu.VMEM((*shape, 8, 128), F32)
        hbm = pl.BlockSpec(memory_space=pltpu.HBM)
        stay = lambda x: pltpu.with_memory_space_constraint(x, pltpu.HBM)
        operands = (target, shape, jnp.transpose(jac, (1, 2, 0, 3)), sensor, shift, weight)
        return pl.pallas_call(
            functools.partial(kernel, n_cond, n_space),
            out_shape=(
                pltpu.VMEM(target.shape, F32),
                pltpu.VMEM((4, rows, 128), F32),
            ),
            in_specs=[hbm] * 6,
            out_specs=(pl.BlockSpec(memory_space=pltpu.VMEM),) * 2,
            scratch_shapes=[
                pltpu.SMEM((3, 5, 2, 5), F32), pltpu.SMEM((2,), F32), pltpu.SMEM((2,), F32),
                vmem(5, 20), vmem(22), vmem(5, 8),
                vmem(21), vmem(4, 20), vmem(20), vmem(20), vmem(75),
                vmem(5, 24), vmem(5, 24), vmem(5, 24), vmem(5, 12), vmem(5, 4),
                vmem(18), vmem(10), vmem(2 * n_cond), vmem(2 * n_cond),
                pltpu.SemaphoreType.DMA((6,)),
                pltpu.SemaphoreType.DMA((64,)),
                pltpu.SemaphoreType.DMA((29,)),
            ],
            compiler_params=pltpu.CompilerParams(
                collective_id=0, has_side_effects=True, vmem_limit_bytes=48 * 2**20
            ),
        )(*map(stay, operands))

    in_specs = (
        P("cond", None, "space", None, None),
        P("cond", None, "space", None, None),
        P("cond", None, None, None),
        P("cond", "space", None, None),
        P("cond"),
        P("cond"),
        P("space", None, None),
        P(None, "space"),
    )
    out_specs = (P("cond", None, "space", None, None), P("space", "cond", None))
    return jax.shard_map(local, mesh=mesh, in_specs=in_specs, out_specs=out_specs, check_vma=False)
```

```python
import functools

import jax
import jax.numpy as jnp
from jax import lax
from jax.experimental import pallas as pl
from jax.experimental.pallas import tpu as pltpu
from jax.sharding import PartitionSpec as P

RELAX = 0.7
EPS = 1.0 / 32.0
F32 = jnp.float32


def sublanes(shape):
    return lax.broadcasted_iota(jnp.int32, shape, len(shape) - 2)


def lanes(shape):
    return lax.broadcasted_iota(jnp.int32, shape, len(shape) - 1)


def up(a, n):
    return pltpu.roll(a, 8 - n, a.ndim - 2)


def down(a, n):
    return pltpu.roll(a, n, a.ndim - 2)


def ahead(a, n):
    return pltpu.roll(a, 128 - n, a.ndim - 1)


def behind(a, n):
    return pltpu.roll(a, n, a.ndim - 1)


def pack(v):
    s, z = sublanes(v[0].shape), lanes(v[0].shape)
    even, low = s % 2 == 0, s % 4 < 2
    zeven, zlow = z % 2 == 0, z % 4 < 2

    def pair(a, b):
        return jnp.where(even, a, b) + jnp.where(even, up(a, 1), down(b, 1))

    def quad(a, b):
        return jnp.where(low, a, b) + jnp.where(low, up(a, 2), down(b, 2))

    four = quad(pair(v[0], v[1]), pair(v[2], v[3]))
    last = pair(v[4], v[4])
    last = quad(last, last)
    both = jnp.where(zeven, four, last) + jnp.where(zeven, ahead(four, 1), behind(last, 1))
    return both + jnp.where(zlow, ahead(both, 2), behind(both, 2))


def unpack(c):
    s, z = sublanes(c.shape), lanes(c.shape)
    even, low, zeven = s % 2 == 0, s % 4 < 2, z % 2 == 0
    four = jnp.where(zeven, c, behind(c, 1))
    last = jnp.where(zeven, ahead(c, 1), c)
    p02 = jnp.where(even, four, down(four, 1))
    p13 = jnp.where(even, up(four, 1), four)
    return (
        jnp.where(low, p02, down(p02, 2)),
        jnp.where(low, p13, down(p13, 2)),
        jnp.where(low, up(p02, 2), p02),
        jnp.where(low, up(p13, 2), p13),
        last,
    )


def neighbours(c, first, last_box):
    own = c[1:-1]
    at = first + lax.broadcasted_iota(jnp.int32, own.shape, 0)
    z = lanes(own.shape)
    total = jnp.where(at == 0, own, c[:-2]) + jnp.where(at == last_box, own, c[2:])
    total = total + (own + up(own, 4))
    return total + jnp.where(z < 4, own, behind(own, 4)) + jnp.where(z >= 124, own, ahead(own, 4))


def coarse_solve(res, first, last_box, inverse):
    scaled = res * inverse
    c = scaled
    for sweep in range(1, 4):
        c = scaled[sweep:-sweep] + 8.0 * inverse * neighbours(c, first + sweep, last_box)
    return c


def coarse_spread(res, first, last_box, inverse):
    none = jnp.zeros((1, 8, 128), F32)
    scaled = res * inverse
    c = scaled
    for sweep in range(1, 4):
        scaled = jnp.concatenate([none, scaled, none])
        c = scaled + 8.0 * inverse * neighbours(jnp.concatenate([none, none, c, none, none]), first - sweep, last_box)
    return c


def off_diagonal(field, at, n, jac, cpx, cyz):
    s, z = sublanes((1, 8, 128)), lanes((1, 8, 128))
    y_not_last, y_not_first = jnp.where(s < 7, 1.0, 0.0), jnp.where(s >= 1, 1.0, 0.0)
    z_not_last, z_not_first = jnp.where(z < 127, 1.0, 0.0), jnp.where(z >= 1, 1.0, 0.0)
    y_far_up, y_far_down = jnp.where(s < 6, -EPS, 0.0), jnp.where(s >= 2, -EPS, 0.0)
    z_far_up, z_far_down = jnp.where(z < 126, -EPS, 0.0), jnp.where(z >= 2, -EPS, 0.0)
    cx = cpx[pl.ds(at - 2, n + 1)]
    cy_plus, cy_minus, cz_plus, cz_minus = (cyz[i, pl.ds(at - 2, n)] for i in range(4))
    center, out = [], [None] * 5

    def add(v, term):
        out[v] = term if out[v] is None else out[v] + term

    for u in range(5):
        block = field[u, pl.ds(at - 2, n + 4)]
        a, plus, minus = block[2:-2], block[3:-1], block[1:-3]
        center.append(a)
        total = cx[1:] * plus
        total = total + cx[:-1] * minus
        total = total - EPS * (block[4:] + block[:-4])
        dx = plus - minus
        plus, minus = up(a, 1), down(a, 1)
        total = total + cy_plus * plus
        total = total + cy_minus * minus
        total = total + y_far_up * up(a, 2)
        total = total + y_far_down * down(a, 2)
        dy = y_not_last * plus - y_not_first * minus
        plus, minus = ahead(a, 1), behind(a, 1)
        total = total + cz_plus * plus
        total = total + cz_minus * minus
        total = total + z_far_up * ahead(a, 2)
        total = total + z_far_down * behind(a, 2)
        dz = z_not_last * plus - z_not_first * minus
        add(u, total)
        for d, diff in enumerate((dx, dy, dz)):
            for v in range(5):
                add(v, jac[d * 25 + u * 5 + v] * diff)
    return center, out


def kernel(
    n_cond, n_space, target_in, shape_in, jac_hbm, sensor_in, shift_hbm, weight_hbm, adjoint_out, sens_out,
    jac_in, shift_in, weight_in, g, sen, shp, cpx, cyz, w, diag, jac, b0, b1, b2, halo, rs, rp1, rp2, sib, cs, rc, local_sem, send_sem, recv_sem, share_sem, known_sem,
):
    space, cond = lax.axis_index("space"), lax.axis_index("cond")
    chip, core = space // 2, space % 2
    chips = n_space // 2
    has_left, has_right = chip > 0, chip < chips - 1
    has_left2, has_right2 = chip > 1, chip < chips - 2
    rows = 8 // n_cond

    ring = [(2 * chip + (core + j) % 2, lax.rem(cond + dz, n_cond)) for dz in range(n_cond) for j in range(2)]
    sibling = 2 * chip + 1 - core
    following, preceding = lax.rem(cond + 1, n_cond), lax.rem(cond + n_cond - 1, n_cond)
    beside = [(2 * (chip + near) + j, cond, there) for near, there in ((-1, has_left), (1, has_right)) for j in range(2)]
    beside += [(sibling, cond, None), (space, following, None), (space, preceding, None)]
    n_beside = 3 + 2 * (has_left.astype(jnp.int32) + has_right.astype(jnp.int32))

    def tell(semaphore, peers):
        for s, c, there in peers:
            def one(s=s, c=c):
                pl.semaphore_signal(semaphore, inc=1, device_id={"space": s, "cond": c})
            one() if there is None else pl.when(there)(one)

    barrier = pltpu.get_barrier_semaphore()
    tell(barrier, beside)

    count = iter(range(1000))
    sends = []

    def remote(src, dst, recv, s, c=cond):
        return pltpu.make_async_remote_copy(
            src_ref=src, dst_ref=dst, send_sem=send_sem.at[next(count)], recv_sem=recv_sem.at[recv],
            device_id={"space": s, "cond": c},
        )

    mine = [
        pltpu.make_async_copy(sensor_in.at[core], sen.at[pl.ds(7 + 4 * core, 4)], local_sem.at[0]),
        pltpu.make_async_copy(target_in.at[core], g.at[:, pl.ds(6 + 4 * core, 4)], local_sem.at[1]),
        pltpu.make_async_copy(shape_in.at[core], shp.at[:, pl.ds(6 + 4 * core, 4)], local_sem.at[2]),
    ]
    small = [
        pltpu.make_async_copy(jac_hbm, jac_in, local_sem.at[3]),
        pltpu.make_async_copy(shift_hbm, shift_in, local_sem.at[4]),
        pltpu.make_async_copy(weight_hbm, weight_in, local_sem.at[5]),
    ]
    for copy in small + mine:
        copy.start()

    pl.semaphore_wait(barrier, n_beside)

    def to_right(k, j):
        low, size, at = ((2, 2, 0), (0, 4, 2))[k]
        s_low, s_size, s_at = ((1, 3, 0), (0, 4, 3))[k]
        there = 2 * (chip + 1) + j
        return [
            remote(sensor_in.at[j, pl.ds(s_low, s_size)], sen.at[pl.ds(s_at, s_size)], 3 + 2 * k, there),
            remote(target_in.at[j, :, pl.ds(low, size)], g.at[:, pl.ds(at, size)], 4 + 2 * k, there),
            remote(shape_in.at[j, :, pl.ds(low, size)], shp.at[:, pl.ds(at, size)], 21 + k, there),
        ]

    def to_left(k, j):
        size, at = ((4, 14), (2, 18))[k]
        s_size, s_at = ((4, 15), (3, 19))[k]
        there = 2 * (chip - 1) + j
        return [
            remote(sensor_in.at[j, pl.ds(0, s_size)], sen.at[pl.ds(s_at, s_size)], 7 + 2 * k, there),
            remote(target_in.at[j, :, pl.ds(0, size)], g.at[:, pl.ds(at, size)], 8 + 2 * k, there),
            remote(shape_in.at[j, :, pl.ds(0, size)], shp.at[:, pl.ds(at, size)], 23 + k, there),
        ]

    first_round = []
    for k in range(2):
        for make, there in ((to_right, has_right), (to_left, has_left)):
            pairs = [make(k, j) for j in range(2)]
            first_round.append(([[c[i] for c in pairs] for i in range(3)], jnp.logical_and(there, core == k)))
    other = 1 - core
    swap = [
        remote(sensor_in.at[other], sen.at[pl.ds(7 + 4 * core, 4)], 0, sibling),
        remote(target_in.at[other], g.at[:, pl.ds(6 + 4 * core, 4)], 1, sibling),
        remote(shape_in.at[other], shp.at[:, pl.ds(6 + 4 * core, 4)], 2, sibling),
    ]
    for copies, there in first_round:
        @pl.when(there)
        def _(copies=copies):
            for copy in copies[0] + copies[1]:
                copy.start()
    for copy in swap[:2]:
        copy.start()
    tell(known_sem.at[0], beside)

    @pl.when(jnp.logical_not(has_left))
    def _():
        g[:, 0:6] = jnp.zeros((5, 6, 8, 128), F32)
        sen[0:7] = jnp.zeros((7, 8, 128), F32)
        halo[:, 0:6] = jnp.zeros((5, 6, 8, 128), F32)
        rp1[3:7] = jnp.zeros((4, 8, 128), F32)
        rp2[:, 0:3] = jnp.zeros((2, 3, 8, 128), F32)
        rc[0] = jnp.zeros(rc.shape[1:], F32)

    @pl.when(jnp.logical_not(has_right))
    def _():
        g[:, 14:20] = jnp.zeros((5, 6, 8, 128), F32)
        sen[15:22] = jnp.zeros((7, 8, 128), F32)
        halo[:, 6:12] = jnp.zeros((5, 6, 8, 128), F32)
        rp1[11:15] = jnp.zeros((4, 8, 128), F32)
        rp2[:, 7:10] = jnp.zeros((2, 3, 8, 128), F32)
        rc[2] = jnp.zeros(rc.shape[1:], F32)

    @pl.when(jnp.logical_not(has_left2))
    def _():
        rp1[0:3] = jnp.zeros((3, 8, 128), F32)

    @pl.when(jnp.logical_not(has_right2))
    def _():
        rp1[15:18] = jnp.zeros((3, 8, 128), F32)

    for copy in small:
        copy.wait()
    for d in range(3):
        for u in range(5):
            for v in range(5):
                jac[d * 25 + u * 5 + v] = jnp.full((8, 128), 0.5 * jac_in[d, u, core, v], F32)
    shift = jnp.full((8, 128), shift_in[core], F32)
    inverse = 1.0 / (shift * 32.0 + 48.0)

    awaited = [(make(k, 0), there) for k in range(2) for make, there in ((to_right, has_left), (to_left, has_right))]

    def arrive_first(i):
        mine[i].wait()
        swap[i].wait_recv()
        for copies, there in awaited:
            pl.when(there)(copies[i].wait_recv)

    arrive_first(0)

    s, z = sublanes((1, 8, 128)), lanes((1, 8, 128))

    def coefficients(k, carry):
        i = 4 * k
        block = sen[pl.ds(i, 6)]
        near = block[1:5]
        x_plus, x_minus = (near + block[2:]) * 0.25, (near + block[:4]) * 0.25
        y_plus = (near + jnp.where(s < 7, up(near, 1), 0.0)) * 0.25
        y_minus = (near + jnp.where(s >= 1, down(near, 1), 0.0)) * 0.25
        z_plus = (near + jnp.where(z < 127, ahead(near, 1), 0.0)) * 0.25
        z_minus = (near + jnp.where(z >= 1, behind(near, 1), 0.0)) * 0.25
        total = shift[None] + ((x_plus + x_minus) + (y_plus + y_minus) + (z_plus + z_minus)) + 18.0 * EPS
        cpx[pl.ds(i + 1, 4)] = x_plus + 4.0 * EPS
        cyz[0, pl.ds(i, 4)] = jnp.where(s < 7, y_plus + 4.0 * EPS, 0.0)
        cyz[1, pl.ds(i, 4)] = jnp.where(s >= 1, y_minus + 4.0 * EPS, 0.0)
        cyz[2, pl.ds(i, 4)] = jnp.where(z < 127, z_plus + 4.0 * EPS, 0.0)
        cyz[3, pl.ds(i, 4)] = jnp.where(z >= 1, z_minus + 4.0 * EPS, 0.0)
        at = i + lax.broadcasted_iota(jnp.int32, total.shape, 0)
        inside = jnp.logical_and(at >= low_layer, at < high_layer)
        diag[pl.ds(i, 4)] = total
        w[pl.ds(i, 4)] = jnp.where(inside, RELAX / total, 0.0)
        return carry

    low_layer, high_layer = jnp.where(has_left, 0, 6), jnp.where(has_right, 20, 14)
    cpx[0:1] = (sen[0:1] + sen[1:2]) * 0.25 + 4.0 * EPS
    lax.fori_loop(0, 5, coefficients, 0)
    arrive_first(1)
    def begin(k, carry):
        i = 4 * k
        weight = w[pl.ds(i, 4)]
        for v in range(5):
            b0[v, pl.ds(i + 2, 4)] = weight * g[v, pl.ds(i, 4)]
        return carry

    lax.fori_loop(0, 5, begin, 0)

    def sweep(src, dst, low, n, times, stride=None):
        def body(i, carry):
            at = low + i * (stride or n)
            center, out = off_diagonal(src, at, n, jac, cpx, cyz)
            weight = w[pl.ds(at - 2, n)]
            for v in range(5):
                dst[v, pl.ds(at, n)] = (1.0 - RELAX) * center[v] + weight * (g[v, pl.ds(at - 2, n)] + out[v])
            return carry

        lax.fori_loop(0, times, body, 0)

    def restrict(src):
        def body(i, carry):
            at = 8 + i * 4
            center, out = off_diagonal(src, at, 4, jac, cpx, cyz)
            d = diag[pl.ds(at - 2, 4)]
            for v in range(5):
                r = g[v, pl.ds(at - 2, 4)] + out[v] - d * center[v]
                rs[v, pl.ds(2 * i, 1)] = r[0:1] + r[1:2]
                rs[v, pl.ds(2 * i + 1, 1)] = r[2:3] + r[3:4]
            return carry

        lax.fori_loop(0, 2, body, 0)
        return pack([rs[v] for v in range(5)])

    right, left = space + 2, space - 2

    def start(copies):
        for copy, there in copies:
            pl.when(there)(copy.start)

    def arrive(copies, theres):
        for (copy, _), there in zip(copies, theres):
            pl.when(there)(copy.wait_recv)

    def sent(copies):
        for copy, there in copies:
            pl.when(there)(copy.wait_send)

    sweep(b0, b1, 4, 4, 4)
    sweep(b1, b0, 6, 4, 3)
    pl.semaphore_wait(known_sem.at[0], n_beside)
    tell(known_sem.at[1], [(space, preceding, None)])
    near_halos = [
        (remote(b0.at[:, pl.ds(12, 2)], halo.at[:, pl.ds(4, 2)], 11, right), has_right),
        (remote(b0.at[:, pl.ds(10, 2)], halo.at[:, pl.ds(6, 2)], 12, left), has_left),
    ]
    far_halos = [
        (remote(b0.at[:, pl.ds(8, 4)], halo.at[:, pl.ds(0, 4)], 19, right), has_right),
        (remote(b0.at[:, pl.ds(12, 4)], halo.at[:, pl.ds(8, 4)], 20, left), has_left),
    ]
    start(near_halos)
    rp1[7:11] = restrict(b0)
    boxes = [
        (remote(rp1.at[pl.ds(8, 3)], rp1.at[pl.ds(0, 3)], 13, space + 4), has_right2),
        (remote(rp1.at[pl.ds(7, 3)], rp1.at[pl.ds(15, 3)], 14, space - 4), has_left2),
        (remote(rp1.at[pl.ds(7, 4)], rp1.at[pl.ds(3, 4)], 15, right), has_right),
        (remote(rp1.at[pl.ds(7, 4)], rp1.at[pl.ds(11, 4)], 16, left), has_left),
    ]
    start(boxes)
    start(far_halos)
    swap[2].start()
    for copies, there in first_round:
        @pl.when(there)
        def _(copies=copies):
            for copy in copies[2]:
                copy.start()

    arrive(boxes, (has_left2, has_right2, has_left, has_right))
    last_box = 4 * chips - 1
    c = coarse_solve(rp1[...], 4 * chip - 7, last_box, inverse[None])
    at = 4 * chip - 4 + lax.broadcasted_iota(jnp.int32, c.shape, 0)
    fixes = unpack(jnp.where(jnp.logical_and(at >= 0, at <= last_box), c, 0.0))

    def correct(old, low, high):
        for v in range(5):
            for i in range(low, high):
                b1[v, i] = old(v, i) + fixes[v][i // 2]

    correct(lambda v, i: b0[v, i], 6, 18)
    sweep(b1, b2, 8, 4, 2)
    arrive(near_halos + far_halos, (has_left, has_right) * 2)
    correct(lambda v, i: halo[v, i], 0, 6)
    correct(lambda v, i: halo[v, i - 12], 18, 24)
    sweep(b1, b2, 2, 6, 2, 14)
    sweep(b2, b1, 4, 4, 4)
    sweep(b1, b2, 6, 4, 3)
    over = remote(b2.at[:, pl.ds(8 + 4 * other, 4)], sib, 25, sibling)
    over.start()
    rp2[core, 3:7] = restrict(b2)

    def boxes_beside(c_at, j):
        return [
            (remote(rp2.at[c_at, pl.ds(4, 3)], rp2.at[c_at, pl.ds(0, 3)], 17 + 9 * c_at, right - core + j), has_right),
            (remote(rp2.at[c_at, pl.ds(3, 3)], rp2.at[c_at, pl.ds(7, 3)], 18 + 9 * c_at, left - core + j), has_left),
        ]

    boxes2 = boxes_beside(core, 0) + boxes_beside(core, 1)
    start(boxes2)
    boxes_over = remote(rp2.at[core, pl.ds(3, 4)], rp2.at[core, pl.ds(3, 4)], 28, sibling)
    boxes_over.start()

    weight = jnp.full((8, 128), weight_in[core], F32)
    mine[2].wait()
    swap[2].wait_recv()
    for copies, there in awaited:
        pl.when(there)(copies[2].wait_recv)
    fixes = unpack(coarse_spread(rp2[core, 3:7], 4 * chip, last_box, inverse[None]))
    parts = []
    for i in range(20):
        total = None
        for v in range(5):
            value = fixes[v][i // 2]
            if 6 <= i < 14:
                value = value + b2[v, 2 + i]
            term = value * shp[v, i]
            total = term if total is None else total + term
        parts.append(weight * total)
    s2 = sublanes((8, 128))
    for d in range(3):
        for j in range(2):
            for c_to in range(n_cond):
                gathered = jnp.zeros((8, 128), F32)
                for i in range(4):
                    at = 8 * d - 2 + 4 * j + i
                    turn = (rows * i - rows * c_to) % 8
                    moved = jnp.zeros((8, 128), F32)
                    if 0 <= at < 20:
                        moved = parts[at] if turn == 0 else down(parts[at], turn)
                    gathered = jnp.where(s2 >= rows * i, moved, gathered) if i else moved
                cs[d, j * n_cond + c_to] = gathered
    me = 2 * cond + core

    def share(d, j, c_to):
        return pltpu.make_async_remote_copy(
            src_ref=cs.at[d, j * n_cond + c_to], dst_ref=rc.at[2 - d, me], send_sem=share_sem.at[d], recv_sem=share_sem.at[5 - d],
            device_id={"space": 2 * (chip + d - 1) + j, "cond": c_to},
        )

    def shared(d, slots):
        return pltpu.make_async_remote_copy(
            src_ref=cs.at[d, pl.ds(0, slots)], dst_ref=rc.at[d, pl.ds(0, slots)], send_sem=share_sem.at[d], recv_sem=share_sem.at[3 + d],
            device_id={"space": sibling, "cond": cond},
        )

    pl.semaphore_wait(known_sem.at[1], 1)
    outer = ((0, has_left), (2, has_right))
    for dz in (2, 1, 3, 0):
        for d, there in outer:
            @pl.when(there)
            def _(d=d, dz=dz):
                for j in range(2):
                    share(d, j, lax.rem(cond + dz, n_cond)).start()
    for s_to, c_to in reversed(ring[1:]):
        share(1, lax.rem(s_to, 2), c_to).start()
    rc[1, me] = cs[1, core * n_cond + cond]

    arrive(boxes_beside(0, 0) + boxes_beside(1, 0), (has_left, has_right) * 2)
    boxes_over.wait_recv()
    over.wait_recv()
    for c_at, old in ((core, lambda v: b2[v, pl.ds(8 + 4 * core, 4)]), (other, lambda v: sib[v])):
        inv = 1.0 / (jnp.full((1, 8, 128), shift_in[c_at], F32) * 32.0 + 48.0)
        c = coarse_solve(rp2[c_at, pl.ds(2 * core, 8)], 4 * chip - 3 + 2 * core, last_box, inv)
        fixes = unpack(c)
        for v in range(5):
            value = old(v)
            for i in range(4):
                adjoint_out[c_at, v, i] = value[i] + fixes[v][i // 2]

    for d, there in outer:
        pl.when(there)(shared(d, 2 * n_cond).wait_recv)
    shared(1, 2 * n_cond - 1).wait_recv()
    total = None
    for d in range(3):
        for i in range(2 * n_cond):
            total = rc[d, i] if total is None else total + rc[d, i]
    for i in range(4):
        sens_out[i] = total[rows * i : rows * (i + 1)]
    over.wait_send()
    boxes_over.wait_send()
    for d, there in outer:
        pl.when(there)(shared(d, 2 * n_cond).wait_send)
    shared(1, 2 * n_cond - 1).wait_send()
    for copy in swap:
        copy.wait_send()
    for copies, there in first_round:
        @pl.when(there)
        def _(copies=copies):
            for copy in copies[0] + copies[1] + copies[2]:
                copy.wait_send()
    sent(near_halos + far_halos + boxes + boxes2)


def solution(mesh):
    n_cond, n_space = mesh.shape["cond"], mesh.shape["space"]
    rows = 8 // n_cond

    def local(target, shape, jac, sensor, shift, weight, agglomeration, links):
        vmem = lambda *shape: pltpu.VMEM((*shape, 8, 128), F32)
        hbm = pl.BlockSpec(memory_space=pltpu.HBM)
        stay = lambda x: pltpu.with_memory_space_constraint(x, pltpu.HBM)
        operands = (target, shape, jnp.transpose(jac, (1, 2, 0, 3)), sensor, shift, weight)
        return pl.pallas_call(
            functools.partial(kernel, n_cond, n_space),
            out_shape=(
                pltpu.VMEM(target.shape, F32),
                pltpu.VMEM((4, rows, 128), F32),
            ),
            in_specs=[hbm] * 6,
            out_specs=(pl.BlockSpec(memory_space=pltpu.VMEM),) * 2,
            scratch_shapes=[
                pltpu.SMEM((3, 5, 2, 5), F32), pltpu.SMEM((2,), F32), pltpu.SMEM((2,), F32),
                vmem(5, 20), vmem(22), vmem(5, 20),
                vmem(21), vmem(4, 20), vmem(20), vmem(20), vmem(75),
                vmem(5, 24), vmem(5, 24), vmem(5, 24), vmem(5, 12), vmem(5, 4),
                vmem(18), vmem(2, 10), vmem(5, 4), vmem(3, 2 * n_cond), vmem(3, 2 * n_cond),
                pltpu.SemaphoreType.DMA((6,)),
                pltpu.SemaphoreType.DMA((64,)),
                pltpu.SemaphoreType.DMA((29,)),
                pltpu.SemaphoreType.DMA((6,)),
                pltpu.SemaphoreType.REGULAR((2,)),
            ],
            compiler_params=pltpu.CompilerParams(
                collective_id=0, has_side_effects=True, vmem_limit_bytes=48 * 2**20
            ),
        )(*map(stay, operands))

    in_specs = (
        P("cond", None, "space", None, None),
        P("cond", None, "space", None, None),
        P("cond", None, None, None),
        P("cond", "space", None, None),
        P("cond"),
        P("cond"),
        P("space", None, None),
        P(None, "space"),
    )
    out_specs = (P("cond", None, "space", None, None), P("space", "cond", None))
    return jax.shard_map(local, mesh=mesh, in_specs=in_specs, out_specs=out_specs, check_vma=False)
```

```python
import functools

import jax
import jax.numpy as jnp
from jax import lax
from jax.experimental import pallas as pl
from jax.experimental.pallas import tpu as pltpu
from jax.sharding import PartitionSpec as P

RELAX = 0.7
EPS = 1.0 / 32.0
F32 = jnp.float32


def sublanes(shape):
    return lax.broadcasted_iota(jnp.int32, shape, len(shape) - 2)


def lanes(shape):
    return lax.broadcasted_iota(jnp.int32, shape, len(shape) - 1)


def up(a, n):
    return pltpu.roll(a, 8 - n, a.ndim - 2)


def down(a, n):
    return pltpu.roll(a, n, a.ndim - 2)


def ahead(a, n):
    return pltpu.roll(a, 128 - n, a.ndim - 1)


def behind(a, n):
    return pltpu.roll(a, n, a.ndim - 1)


def pack(v):
    s, z = sublanes(v[0].shape), lanes(v[0].shape)
    even, low = s % 2 == 0, s % 4 < 2
    zeven, zlow = z % 2 == 0, z % 4 < 2

    def pair(a, b):
        return jnp.where(even, a, b) + jnp.where(even, up(a, 1), down(b, 1))

    def quad(a, b):
        return jnp.where(low, a, b) + jnp.where(low, up(a, 2), down(b, 2))

    four = quad(pair(v[0], v[1]), pair(v[2], v[3]))
    last = pair(v[4], v[4])
    last = quad(last, last)
    both = jnp.where(zeven, four, last) + jnp.where(zeven, ahead(four, 1), behind(last, 1))
    return both + jnp.where(zlow, ahead(both, 2), behind(both, 2))


def unpack(c):
    s, z = sublanes(c.shape), lanes(c.shape)
    even, low, zeven = s % 2 == 0, s % 4 < 2, z % 2 == 0
    four = jnp.where(zeven, c, behind(c, 1))
    last = jnp.where(zeven, ahead(c, 1), c)
    p02 = jnp.where(even, four, down(four, 1))
    p13 = jnp.where(even, up(four, 1), four)
    return (
        jnp.where(low, p02, down(p02, 2)),
        jnp.where(low, p13, down(p13, 2)),
        jnp.where(low, up(p02, 2), p02),
        jnp.where(low, up(p13, 2), p13),
        last,
    )


def neighbours(c, first, last_box):
    own = c[1:-1]
    at = first + lax.broadcasted_iota(jnp.int32, own.shape, 0)
    z = lanes(own.shape)
    total = jnp.where(at == 0, own, c[:-2]) + jnp.where(at == last_box, own, c[2:])
    total = total + (own + up(own, 4))
    return total + jnp.where(z < 4, own, behind(own, 4)) + jnp.where(z >= 124, own, ahead(own, 4))


def coarse_solve(res, first, last_box, inverse):
    scaled = res * inverse
    c = scaled
    for sweep in range(1, 4):
        c = scaled[sweep:-sweep] + 8.0 * inverse * neighbours(c, first + sweep, last_box)
    return c


def coarse_spread(res, first, last_box, inverse):
    none = jnp.zeros((1, 8, 128), F32)
    scaled = res * inverse
    c = scaled
    for sweep in range(1, 4):
        scaled = jnp.concatenate([none, scaled, none])
        c = scaled + 8.0 * inverse * neighbours(jnp.concatenate([none, none, c, none, none]), first - sweep, last_box)
    return c


def off_diagonal(field, at, n, jac, cpx, cyz):
    s, z = sublanes((1, 8, 128)), lanes((1, 8, 128))
    y_not_last, y_not_first = jnp.where(s < 7, 1.0, 0.0), jnp.where(s >= 1, 1.0, 0.0)
    z_not_last, z_not_first = jnp.where(z < 127, 1.0, 0.0), jnp.where(z >= 1, 1.0, 0.0)
    y_far_up, y_far_down = jnp.where(s < 6, -EPS, 0.0), jnp.where(s >= 2, -EPS, 0.0)
    z_far_up, z_far_down = jnp.where(z < 126, -EPS, 0.0), jnp.where(z >= 2, -EPS, 0.0)
    cx = cpx[pl.ds(at - 2, n + 1)]
    cy_plus, cy_minus, cz_plus, cz_minus = (cyz[i, pl.ds(at - 2, n)] for i in range(4))
    center, out = [], [None] * 5

    def add(v, term):
        out[v] = term if out[v] is None else out[v] + term

    for u in range(5):
        block = field[u, pl.ds(at - 2, n + 4)]
        a, plus, minus = block[2:-2], block[3:-1], block[1:-3]
        center.append(a)
        total = cx[1:] * plus
        total = total + cx[:-1] * minus
        total = total - EPS * (block[4:] + block[:-4])
        dx = plus - minus
        plus, minus = up(a, 1), down(a, 1)
        total = total + cy_plus * plus
        total = total + cy_minus * minus
        total = total + y_far_up * up(a, 2)
        total = total + y_far_down * down(a, 2)
        dy = y_not_last * plus - y_not_first * minus
        plus, minus = ahead(a, 1), behind(a, 1)
        total = total + cz_plus * plus
        total = total + cz_minus * minus
        total = total + z_far_up * ahead(a, 2)
        total = total + z_far_down * behind(a, 2)
        dz = z_not_last * plus - z_not_first * minus
        add(u, total)
        for d, diff in enumerate((dx, dy, dz)):
            for v in range(5):
                add(v, jac[d * 25 + u * 5 + v] * diff)
    return center, out


def kernel(
    n_cond, n_space, target_in, shape_in, jac_hbm, sensor_in, shift_hbm, weight_hbm, adjoint_out, sens_out,
    jac_in, shift_in, weight_in, g, sen, shp, cpx, cyz, w, diag, jac, b0, b1, b2, halo, rs, rp1, rp2, sib, cs, rc, local_sem, send_sem, recv_sem, share_sem, known_sem,
):
    space, cond = lax.axis_index("space"), lax.axis_index("cond")
    chip, core = space // 2, space % 2
    chips = n_space // 2
    has_left, has_right = chip > 0, chip < chips - 1
    has_left2, has_right2 = chip > 1, chip < chips - 2
    rows = 8 // n_cond

    ring = [(2 * chip + (core + j) % 2, lax.rem(cond + dz, n_cond)) for dz in range(n_cond) for j in range(2)]
    sibling = 2 * chip + 1 - core
    following, preceding = lax.rem(cond + 1, n_cond), lax.rem(cond + n_cond - 1, n_cond)
    beside = [(2 * (chip + near) + j, cond, there) for near, there in ((-1, has_left), (1, has_right)) for j in range(2)]
    beside += [(sibling, cond, None), (space, following, None), (space, preceding, None)]
    n_beside = 3 + 2 * (has_left.astype(jnp.int32) + has_right.astype(jnp.int32))

    def tell(semaphore, peers):
        for s, c, there in peers:
            def one(s=s, c=c):
                pl.semaphore_signal(semaphore, inc=1, device_id={"space": s, "cond": c})
            one() if there is None else pl.when(there)(one)

    barrier = pltpu.get_barrier_semaphore()
    tell(barrier, beside)

    count = iter(range(1000))
    sends = []

    def remote(src, dst, recv, s, c=cond):
        return pltpu.make_async_remote_copy(
            src_ref=src, dst_ref=dst, send_sem=send_sem.at[next(count)], recv_sem=recv_sem.at[recv],
            device_id={"space": s, "cond": c},
        )

    mine = [
        pltpu.make_async_copy(sensor_in.at[core], sen.at[pl.ds(7 + 4 * core, 4)], local_sem.at[0]),
        pltpu.make_async_copy(target_in.at[core], g.at[:, pl.ds(6 + 4 * core, 4)], local_sem.at[1]),
        pltpu.make_async_copy(shape_in.at[core], shp.at[:, pl.ds(6 + 4 * core, 4)], local_sem.at[2]),
    ]
    small = [
        pltpu.make_async_copy(jac_hbm, jac_in, local_sem.at[3]),
        pltpu.make_async_copy(shift_hbm, shift_in, local_sem.at[4]),
        pltpu.make_async_copy(weight_hbm, weight_in, local_sem.at[5]),
    ]
    for copy in small + mine:
        copy.start()

    pl.semaphore_wait(barrier, n_beside)

    def to_right(k, j):
        low, size, at = ((2, 2, 0), (0, 4, 2))[k]
        s_low, s_size, s_at = ((1, 3, 0), (0, 4, 3))[k]
        there = 2 * (chip + 1) + j
        return [
            remote(sensor_in.at[j, pl.ds(s_low, s_size)], sen.at[pl.ds(s_at, s_size)], 3 + 2 * k, there),
            remote(target_in.at[j, :, pl.ds(low, size)], g.at[:, pl.ds(at, size)], 4 + 2 * k, there),
            remote(shape_in.at[j, :, pl.ds(low, size)], shp.at[:, pl.ds(at, size)], 21 + k, there),
        ]

    def to_left(k, j):
        size, at = ((4, 14), (2, 18))[k]
        s_size, s_at = ((4, 15), (3, 19))[k]
        there = 2 * (chip - 1) + j
        return [
            remote(sensor_in.at[j, pl.ds(0, s_size)], sen.at[pl.ds(s_at, s_size)], 7 + 2 * k, there),
            remote(target_in.at[j, :, pl.ds(0, size)], g.at[:, pl.ds(at, size)], 8 + 2 * k, there),
            remote(shape_in.at[j, :, pl.ds(0, size)], shp.at[:, pl.ds(at, size)], 23 + k, there),
        ]

    first_round = []
    for near in (True, False):
        for make, there, k in ((to_right, has_right, 1 if near else 0), (to_left, has_left, 0 if near else 1)):
            pairs = [make(k, j) for j in range(2)]
            first_round.append(([[c[i] for c in pairs] for i in range(3)], jnp.logical_and(there, core == k)))
    other = 1 - core
    swap = [
        remote(sensor_in.at[other], sen.at[pl.ds(7 + 4 * core, 4)], 0, sibling),
        remote(target_in.at[other], g.at[:, pl.ds(6 + 4 * core, 4)], 1, sibling),
        remote(shape_in.at[other], shp.at[:, pl.ds(6 + 4 * core, 4)], 2, sibling),
    ]
    def send_first(items):
        for copies, there in items:
            @pl.when(there)
            def _(copies=copies):
                for copy in copies[0] + copies[1]:
                    copy.start()

    send_first(first_round[:2])
    for copy in swap[:2]:
        copy.start()
    send_first(first_round[2:])
    tell(known_sem.at[0], beside)

    @pl.when(jnp.logical_not(has_left))
    def _():
        g[:, 0:6] = jnp.zeros((5, 6, 8, 128), F32)
        sen[0:7] = jnp.zeros((7, 8, 128), F32)
        halo[:, 0:6] = jnp.zeros((5, 6, 8, 128), F32)
        rp1[3:7] = jnp.zeros((4, 8, 128), F32)
        rp2[:, 0:3] = jnp.zeros((2, 3, 8, 128), F32)
        rc[0] = jnp.zeros(rc.shape[1:], F32)

    @pl.when(jnp.logical_not(has_right))
    def _():
        g[:, 14:20] = jnp.zeros((5, 6, 8, 128), F32)
        sen[15:22] = jnp.zeros((7, 8, 128), F32)
        halo[:, 6:12] = jnp.zeros((5, 6, 8, 128), F32)
        rp1[11:15] = jnp.zeros((4, 8, 128), F32)
        rp2[:, 7:10] = jnp.zeros((2, 3, 8, 128), F32)
        rc[2] = jnp.zeros(rc.shape[1:], F32)

    @pl.when(jnp.logical_not(has_left2))
    def _():
        rp1[0:3] = jnp.zeros((3, 8, 128), F32)

    @pl.when(jnp.logical_not(has_right2))
    def _():
        rp1[15:18] = jnp.zeros((3, 8, 128), F32)

    for copy in small:
        copy.wait()
    for d in range(3):
        for u in range(5):
            for v in range(5):
                jac[d * 25 + u * 5 + v] = jnp.full((8, 128), 0.5 * jac_in[d, u, core, v], F32)
    shift = jnp.full((8, 128), shift_in[core], F32)
    inverse = 1.0 / (shift * 32.0 + 48.0)

    from_left, from_right = ([make(k, 0) for k in range(2)] for make in (to_right, to_left))

    def arrive_first(i, copies, there):
        @pl.when(there)
        def _():
            for copy in copies:
                copy[i].wait_recv()

    mine[0].wait()
    swap[0].wait_recv()
    arrive_first(0, from_left, has_left)

    s, z = sublanes((1, 8, 128)), lanes((1, 8, 128))

    def coefficients(k, carry):
        i = 4 * k
        block = sen[pl.ds(i, 6)]
        near = block[1:5]
        x_plus, x_minus = (near + block[2:]) * 0.25, (near + block[:4]) * 0.25
        y_plus = (near + jnp.where(s < 7, up(near, 1), 0.0)) * 0.25
        y_minus = (near + jnp.where(s >= 1, down(near, 1), 0.0)) * 0.25
        z_plus = (near + jnp.where(z < 127, ahead(near, 1), 0.0)) * 0.25
        z_minus = (near + jnp.where(z >= 1, behind(near, 1), 0.0)) * 0.25
        total = shift[None] + ((x_plus + x_minus) + (y_plus + y_minus) + (z_plus + z_minus)) + 18.0 * EPS
        cpx[pl.ds(i + 1, 4)] = x_plus + 4.0 * EPS
        cyz[0, pl.ds(i, 4)] = jnp.where(s < 7, y_plus + 4.0 * EPS, 0.0)
        cyz[1, pl.ds(i, 4)] = jnp.where(s >= 1, y_minus + 4.0 * EPS, 0.0)
        cyz[2, pl.ds(i, 4)] = jnp.where(z < 127, z_plus + 4.0 * EPS, 0.0)
        cyz[3, pl.ds(i, 4)] = jnp.where(z >= 1, z_minus + 4.0 * EPS, 0.0)
        at = i + lax.broadcasted_iota(jnp.int32, total.shape, 0)
        inside = jnp.logical_and(at >= low_layer, at < high_layer)
        diag[pl.ds(i, 4)] = total
        w[pl.ds(i, 4)] = jnp.where(inside, RELAX / total, 0.0)
        return carry

    low_layer, high_layer = jnp.where(has_left, 0, 6), jnp.where(has_right, 20, 14)
    cpx[0:1] = (sen[0:1] + sen[1:2]) * 0.25 + 4.0 * EPS
    lax.fori_loop(0, 3, coefficients, 0)

    def begin(k, carry):
        i = 4 * k
        weight = w[pl.ds(i, 4)]
        for v in range(5):
            b0[v, pl.ds(i + 2, 4)] = weight * g[v, pl.ds(i, 4)]
        return carry

    def sweep(src, dst, low, n, times, stride=None):
        def body(i, carry):
            at = low + i * (stride or n)
            center, out = off_diagonal(src, at, n, jac, cpx, cyz)
            weight = w[pl.ds(at - 2, n)]
            for v in range(5):
                dst[v, pl.ds(at, n)] = (1.0 - RELAX) * center[v] + weight * (g[v, pl.ds(at - 2, n)] + out[v])
            return carry

        lax.fori_loop(0, times, body, 0)

    def restrict(src):
        def body(i, carry):
            at = 8 + i * 4
            center, out = off_diagonal(src, at, 4, jac, cpx, cyz)
            d = diag[pl.ds(at - 2, 4)]
            for v in range(5):
                r = g[v, pl.ds(at - 2, 4)] + out[v] - d * center[v]
                rs[v, pl.ds(2 * i, 1)] = r[0:1] + r[1:2]
                rs[v, pl.ds(2 * i + 1, 1)] = r[2:3] + r[3:4]
            return carry

        lax.fori_loop(0, 2, body, 0)
        return pack([rs[v] for v in range(5)])

    right, left = space + 2, space - 2

    def start(copies):
        for copy, there in copies:
            pl.when(there)(copy.start)

    def arrive(copies, theres):
        for (copy, _), there in zip(copies, theres):
            pl.when(there)(copy.wait_recv)

    def sent(copies):
        for copy, there in copies:
            pl.when(there)(copy.wait_send)

    mine[1].wait()
    swap[1].wait_recv()
    arrive_first(1, from_left, has_left)
    lax.fori_loop(0, 3, begin, 0)
    sweep(b0, b1, 4, 4, 2)
    sweep(b1, b2, 6, 4, 1)
    arrive_first(0, from_right, has_right)
    lax.fori_loop(3, 5, coefficients, 0)
    arrive_first(1, from_right, has_right)
    lax.fori_loop(3, 5, begin, 0)
    sweep(b0, b1, 12, 4, 2)
    sweep(b1, b2, 10, 4, 2)
    pl.semaphore_wait(known_sem.at[0], n_beside)
    tell(known_sem.at[1], [(space, preceding, None)])
    near_halos = [
        (remote(b2.at[:, pl.ds(12, 2)], halo.at[:, pl.ds(4, 2)], 11, right), has_right),
        (remote(b2.at[:, pl.ds(10, 2)], halo.at[:, pl.ds(6, 2)], 12, left), has_left),
    ]
    far_halos = [
        (remote(b2.at[:, pl.ds(8, 4)], halo.at[:, pl.ds(0, 4)], 19, right), has_right),
        (remote(b2.at[:, pl.ds(12, 4)], halo.at[:, pl.ds(8, 4)], 20, left), has_left),
    ]
    start(near_halos)
    rp1[7:11] = restrict(b2)
    boxes = [
        (remote(rp1.at[pl.ds(7, 4)], rp1.at[pl.ds(3, 4)], 15, right), has_right),
        (remote(rp1.at[pl.ds(7, 4)], rp1.at[pl.ds(11, 4)], 16, left), has_left),
        (remote(rp1.at[pl.ds(8, 3)], rp1.at[pl.ds(0, 3)], 13, space + 4), has_right2),
        (remote(rp1.at[pl.ds(7, 3)], rp1.at[pl.ds(15, 3)], 14, space - 4), has_left2),
    ]
    start(boxes)
    start(far_halos)
    swap[2].start()
    for copies, there in first_round:
        @pl.when(there)
        def _(copies=copies):
            for copy in copies[2]:
                copy.start()

    arrive(boxes, (has_left, has_right, has_left2, has_right2))
    last_box = 4 * chips - 1
    c = coarse_solve(rp1[...], 4 * chip - 7, last_box, inverse[None])
    at = 4 * chip - 4 + lax.broadcasted_iota(jnp.int32, c.shape, 0)
    fixes = unpack(jnp.where(jnp.logical_and(at >= 0, at <= last_box), c, 0.0))

    def correct(old, low, high):
        for v in range(5):
            for i in range(low, high):
                b1[v, i] = old(v, i) + fixes[v][i // 2]

    correct(lambda v, i: b2[v, i], 6, 18)
    sweep(b1, b0, 8, 4, 2)
    arrive(near_halos + far_halos, (has_left, has_right) * 2)
    correct(lambda v, i: halo[v, i], 0, 6)
    correct(lambda v, i: halo[v, i - 12], 18, 24)
    sweep(b1, b0, 2, 6, 2, 14)
    sweep(b0, b1, 4, 4, 4)
    sweep(b1, b0, 6, 4, 3)
    over = remote(b0.at[:, pl.ds(8 + 4 * other, 4)], sib, 25, sibling)
    over.start()
    rp2[core, 3:7] = restrict(b0)

    def boxes_beside(c_at, j):
        return [
            (remote(rp2.at[c_at, pl.ds(4, 3)], rp2.at[c_at, pl.ds(0, 3)], 17 + 9 * c_at, right - core + j), has_right),
            (remote(rp2.at[c_at, pl.ds(3, 3)], rp2.at[c_at, pl.ds(7, 3)], 18 + 9 * c_at, left - core + j), has_left),
        ]

    boxes2 = boxes_beside(core, 0) + boxes_beside(core, 1)

    weight = jnp.full((8, 128), weight_in[core], F32)
    mine[2].wait()
    swap[2].wait_recv()
    arrive_first(2, from_left, has_left)
    arrive_first(2, from_right, has_right)
    fixes = unpack(coarse_spread(rp2[core, 3:7], 4 * chip, last_box, inverse[None]))
    parts = []
    for i in range(20):
        total = None
        for v in range(5):
            value = fixes[v][i // 2]
            if 6 <= i < 14:
                value = value + b0[v, 2 + i]
            term = value * shp[v, i]
            total = term if total is None else total + term
        parts.append(weight * total)
    s2 = sublanes((8, 128))
    for d in range(3):
        for j in range(2):
            for c_to in range(n_cond):
                gathered = jnp.zeros((8, 128), F32)
                for i in range(4):
                    at = 8 * d - 2 + 4 * j + i
                    turn = (rows * i - rows * c_to) % 8
                    moved = jnp.zeros((8, 128), F32)
                    if 0 <= at < 20:
                        moved = parts[at] if turn == 0 else down(parts[at], turn)
                    gathered = jnp.where(s2 >= rows * i, moved, gathered) if i else moved
                cs[d, j * n_cond + c_to] = gathered
    me = 2 * cond + core

    def share(d, j, c_to):
        return pltpu.make_async_remote_copy(
            src_ref=cs.at[d, j * n_cond + c_to], dst_ref=rc.at[2 - d, me], send_sem=share_sem.at[d], recv_sem=share_sem.at[5 - d],
            device_id={"space": 2 * (chip + d - 1) + j, "cond": c_to},
        )

    def shared(d, slots):
        return pltpu.make_async_remote_copy(
            src_ref=cs.at[d, pl.ds(0, slots)], dst_ref=rc.at[d, pl.ds(0, slots)], send_sem=share_sem.at[d], recv_sem=share_sem.at[3 + d],
            device_id={"space": sibling, "cond": cond},
        )

    pl.semaphore_wait(known_sem.at[1], 1)
    outer = ((0, has_left), (2, has_right))
    for dz in (2, 1, 3, 0):
        for d, there in outer:
            @pl.when(there)
            def _(d=d, dz=dz):
                for j in range(2):
                    share(d, j, lax.rem(cond + dz, n_cond)).start()
    for s_to, c_to in reversed(ring[1:]):
        share(1, lax.rem(s_to, 2), c_to).start()
    rc[1, me] = cs[1, core * n_cond + cond]

    start(boxes2)
    boxes_over = remote(rp2.at[core, pl.ds(3, 4)], rp2.at[core, pl.ds(3, 4)], 28, sibling)
    boxes_over.start()

    arrive(boxes_beside(0, 0) + boxes_beside(1, 0), (has_left, has_right) * 2)
    boxes_over.wait_recv()
    over.wait_recv()
    for c_at, old in ((core, lambda v: b0[v, pl.ds(8 + 4 * core, 4)]), (other, lambda v: sib[v])):
        inv = 1.0 / (jnp.full((1, 8, 128), shift_in[c_at], F32) * 32.0 + 48.0)
        c = coarse_solve(rp2[c_at, pl.ds(2 * core, 8)], 4 * chip - 3 + 2 * core, last_box, inv)
        fixes = unpack(c)
        for v in range(5):
            value = old(v)
            for i in range(4):
                adjoint_out[c_at, v, i] = value[i] + fixes[v][i // 2]

    for d, there in outer:
        pl.when(there)(shared(d, 2 * n_cond).wait_recv)
    shared(1, 2 * n_cond - 1).wait_recv()
    total = None
    for d in range(3):
        for i in range(2 * n_cond):
            total = rc[d, i] if total is None else total + rc[d, i]
    for i in range(4):
        sens_out[i] = total[rows * i : rows * (i + 1)]
    over.wait_send()
    boxes_over.wait_send()
    for d, there in outer:
        pl.when(there)(shared(d, 2 * n_cond).wait_send)
    shared(1, 2 * n_cond - 1).wait_send()
    for copy in swap:
        copy.wait_send()
    for copies, there in first_round:
        @pl.when(there)
        def _(copies=copies):
            for copy in copies[0] + copies[1] + copies[2]:
                copy.wait_send()
    sent(near_halos + far_halos + boxes + boxes2)


def settle(adjoint, sens, adjoint_out, sens_out, sem):
    copies = [pltpu.make_async_copy(adjoint, adjoint_out, sem.at[0]), pltpu.make_async_copy(sens, sens_out, sem.at[1])]
    for copy in copies:
        copy.start()
    for copy in copies:
        copy.wait()


def solution(mesh):
    n_cond, n_space = mesh.shape["cond"], mesh.shape["space"]
    rows = 8 // n_cond

    def local(target, shape, jac, sensor, shift, weight, agglomeration, links):
        vmem = lambda *shape: pltpu.VMEM((*shape, 8, 128), F32)
        hbm = pl.BlockSpec(memory_space=pltpu.HBM)
        stay = lambda x: pltpu.with_memory_space_constraint(x, pltpu.HBM)
        operands = (target, shape, jnp.transpose(jac, (1, 2, 0, 3)), sensor, shift, weight)
        adjoint, sens = pl.pallas_call(
            functools.partial(kernel, n_cond, n_space),
            out_shape=(
                pltpu.VMEM(target.shape, F32),
                pltpu.VMEM((4, rows, 128), F32),
            ),
            in_specs=[hbm] * 6,
            out_specs=(pl.BlockSpec(memory_space=pltpu.VMEM),) * 2,
            scratch_shapes=[
                pltpu.SMEM((3, 5, 2, 5), F32), pltpu.SMEM((2,), F32), pltpu.SMEM((2,), F32),
                vmem(5, 20), vmem(22), vmem(5, 20),
                vmem(21), vmem(4, 20), vmem(20), vmem(20), vmem(75),
                vmem(5, 24), vmem(5, 24), vmem(5, 24), vmem(5, 12), vmem(5, 4),
                vmem(18), vmem(2, 10), vmem(5, 4), vmem(3, 2 * n_cond), vmem(3, 2 * n_cond),
                pltpu.SemaphoreType.DMA((6,)),
                pltpu.SemaphoreType.DMA((64,)),
                pltpu.SemaphoreType.DMA((29,)),
                pltpu.SemaphoreType.DMA((6,)),
                pltpu.SemaphoreType.REGULAR((2,)),
            ],
            compiler_params=pltpu.CompilerParams(
                collective_id=0, has_side_effects=True, vmem_limit_bytes=48 * 2**20
            ),
        )(*map(stay, operands))
        return pl.pallas_call(
            settle,
            out_shape=(pltpu.HBM(adjoint.shape, F32), pltpu.HBM(sens.shape, F32)),
            in_specs=[pl.BlockSpec(memory_space=pltpu.VMEM)] * 2,
            out_specs=(hbm, hbm),
            scratch_shapes=[pltpu.SemaphoreType.DMA((2,))],
        )(*(pltpu.with_memory_space_constraint(x, pltpu.VMEM) for x in (adjoint, sens)))

    in_specs = (
        P("cond", None, "space", None, None),
        P("cond", None, "space", None, None),
        P("cond", None, None, None),
        P("cond", "space", None, None),
        P("cond"),
        P("cond"),
        P("space", None, None),
        P(None, "space"),
    )
    out_specs = (P("cond", None, "space", None, None), P("space", "cond", None))
    return jax.shard_map(local, mesh=mesh, in_specs=in_specs, out_specs=out_specs, check_vma=False)
```

```python
import functools

import jax
import jax.numpy as jnp
from jax import lax
from jax.experimental import pallas as pl
from jax.experimental.pallas import tpu as pltpu
from jax.sharding import PartitionSpec as P

RELAX = 0.7
EPS = 1.0 / 32.0
F32 = jnp.float32


def sublanes(shape):
    return lax.broadcasted_iota(jnp.int32, shape, len(shape) - 2)


def lanes(shape):
    return lax.broadcasted_iota(jnp.int32, shape, len(shape) - 1)


def up(a, n):
    return pltpu.roll(a, 8 - n, a.ndim - 2)


def down(a, n):
    return pltpu.roll(a, n, a.ndim - 2)


def ahead(a, n):
    return pltpu.roll(a, 128 - n, a.ndim - 1)


def behind(a, n):
    return pltpu.roll(a, n, a.ndim - 1)


def pack(v):
    s, z = sublanes(v[0].shape), lanes(v[0].shape)
    even, low = s % 2 == 0, s % 4 < 2
    zeven, zlow = z % 2 == 0, z % 4 < 2

    def pair(a, b):
        return jnp.where(even, a, b) + jnp.where(even, up(a, 1), down(b, 1))

    def quad(a, b):
        return jnp.where(low, a, b) + jnp.where(low, up(a, 2), down(b, 2))

    four = quad(pair(v[0], v[1]), pair(v[2], v[3]))
    last = pair(v[4], v[4])
    last = quad(last, last)
    both = jnp.where(zeven, four, last) + jnp.where(zeven, ahead(four, 1), behind(last, 1))
    return both + jnp.where(zlow, ahead(both, 2), behind(both, 2))


def unpack(c):
    s, z = sublanes(c.shape), lanes(c.shape)
    even, low, zeven = s % 2 == 0, s % 4 < 2, z % 2 == 0
    four = jnp.where(zeven, c, behind(c, 1))
    last = jnp.where(zeven, ahead(c, 1), c)
    p02 = jnp.where(even, four, down(four, 1))
    p13 = jnp.where(even, up(four, 1), four)
    return (
        jnp.where(low, p02, down(p02, 2)),
        jnp.where(low, p13, down(p13, 2)),
        jnp.where(low, up(p02, 2), p02),
        jnp.where(low, up(p13, 2), p13),
        last,
    )


def neighbours(c, first, last_box):
    own = c[1:-1]
    at = first + lax.broadcasted_iota(jnp.int32, own.shape, 0)
    z = lanes(own.shape)
    total = jnp.where(at == 0, own, c[:-2]) + jnp.where(at == last_box, own, c[2:])
    total = total + (own + up(own, 4))
    return total + jnp.where(z < 4, own, behind(own, 4)) + jnp.where(z >= 124, own, ahead(own, 4))


def coarse_solve(res, first, last_box, inverse):
    scaled = res * inverse
    c = scaled
    for sweep in range(1, 4):
        c = scaled[sweep:-sweep] + 8.0 * inverse * neighbours(c, first + sweep, last_box)
    return c


def coarse_spread(res, first, last_box, inverse):
    none = jnp.zeros((1, 8, 128), F32)
    scaled = res * inverse
    c = scaled
    for sweep in range(1, 4):
        scaled = jnp.concatenate([none, scaled, none])
        c = scaled + 8.0 * inverse * neighbours(jnp.concatenate([none, none, c, none, none]), first - sweep, last_box)
    return c


def off_diagonal(field, at, n, jac, cpx, cyz):
    s, z = sublanes((1, 8, 128)), lanes((1, 8, 128))
    y_not_last, y_not_first = jnp.where(s < 7, 1.0, 0.0), jnp.where(s >= 1, 1.0, 0.0)
    z_not_last, z_not_first = jnp.where(z < 127, 1.0, 0.0), jnp.where(z >= 1, 1.0, 0.0)
    y_far_up, y_far_down = jnp.where(s < 6, -EPS, 0.0), jnp.where(s >= 2, -EPS, 0.0)
    z_far_up, z_far_down = jnp.where(z < 126, -EPS, 0.0), jnp.where(z >= 2, -EPS, 0.0)
    cx = cpx[pl.ds(at - 2, n + 1)]
    cy_plus, cy_minus, cz_plus, cz_minus = (cyz[i, pl.ds(at - 2, n)] for i in range(4))
    center, out = [], [None] * 5

    def add(v, term):
        out[v] = term if out[v] is None else out[v] + term

    for u in range(5):
        block = field[u, pl.ds(at - 2, n + 4)]
        a, plus, minus = block[2:-2], block[3:-1], block[1:-3]
        center.append(a)
        total = cx[1:] * plus
        total = total + cx[:-1] * minus
        total = total - EPS * (block[4:] + block[:-4])
        dx = plus - minus
        plus, minus = up(a, 1), down(a, 1)
        total = total + cy_plus * plus
        total = total + cy_minus * minus
        total = total + y_far_up * up(a, 2)
        total = total + y_far_down * down(a, 2)
        dy = y_not_last * plus - y_not_first * minus
        plus, minus = ahead(a, 1), behind(a, 1)
        total = total + cz_plus * plus
        total = total + cz_minus * minus
        total = total + z_far_up * ahead(a, 2)
        total = total + z_far_down * behind(a, 2)
        dz = z_not_last * plus - z_not_first * minus
        add(u, total)
        for d, diff in enumerate((dx, dy, dz)):
            for v in range(5):
                add(v, jac[d * 25 + u * 5 + v] * diff)
    return center, out


def kernel(
    n_cond, n_space, target_in, shape_in, jac_hbm, sensor_in, shift_hbm, weight_hbm, adjoint_out, sens_out,
    jac_in, shift_in, weight_in, g, sen, shp, cpx, cyz, w, diag, jac, b0, b1, b2, halo, rs, rp1, rp2, sib, cs, rc, local_sem, send_sem, recv_sem, share_sem, known_sem,
):
    space, cond = lax.axis_index("space"), lax.axis_index("cond")
    chip, core = space // 2, space % 2
    chips = n_space // 2
    has_left, has_right = chip > 0, chip < chips - 1
    has_left2, has_right2 = chip > 1, chip < chips - 2
    rows = 8 // n_cond

    ring = [(2 * chip + (core + j) % 2, lax.rem(cond + dz, n_cond)) for dz in range(n_cond) for j in range(2)]
    sibling = 2 * chip + 1 - core
    following, preceding = lax.rem(cond + 1, n_cond), lax.rem(cond + n_cond - 1, n_cond)
    beside = [(2 * (chip + near) + j, cond, there) for near, there in ((-1, has_left), (1, has_right)) for j in range(2)]
    beside += [(sibling, cond, None), (space, following, None), (space, preceding, None)]
    n_beside = 3 + 2 * (has_left.astype(jnp.int32) + has_right.astype(jnp.int32))

    def tell(semaphore, peers):
        for s, c, there in peers:
            def one(s=s, c=c):
                pl.semaphore_signal(semaphore, inc=1, device_id={"space": s, "cond": c})
            one() if there is None else pl.when(there)(one)

    barrier = pltpu.get_barrier_semaphore()
    tell(barrier, beside)

    count = iter(range(1000))
    sends = []

    def remote(src, dst, recv, s, c=cond):
        return pltpu.make_async_remote_copy(
            src_ref=src, dst_ref=dst, send_sem=send_sem.at[next(count)], recv_sem=recv_sem.at[recv],
            device_id={"space": s, "cond": c},
        )

    mine = [
        pltpu.make_async_copy(sensor_in.at[core], sen.at[pl.ds(7 + 4 * core, 4)], local_sem.at[0]),
        pltpu.make_async_copy(target_in.at[core], g.at[:, pl.ds(6 + 4 * core, 4)], local_sem.at[1]),
        pltpu.make_async_copy(shape_in.at[core], shp.at[:, pl.ds(6 + 4 * core, 4)], local_sem.at[2]),
    ]
    small = [
        pltpu.make_async_copy(jac_hbm, jac_in, local_sem.at[3]),
        pltpu.make_async_copy(shift_hbm, shift_in, local_sem.at[4]),
        pltpu.make_async_copy(weight_hbm, weight_in, local_sem.at[5]),
    ]
    for copy in small + mine:
        copy.start()

    pl.semaphore_wait(barrier, n_beside)

    def to_right(k, j):
        low, size, at = ((2, 2, 0), (0, 4, 2))[k]
        s_low, s_size, s_at = ((1, 3, 0), (0, 4, 3))[k]
        there = 2 * (chip + 1) + j
        return [
            remote(sensor_in.at[j, pl.ds(s_low, s_size)], sen.at[pl.ds(s_at, s_size)], 3 + 2 * k, there),
            remote(target_in.at[j, :, pl.ds(low, size)], g.at[:, pl.ds(at, size)], 4 + 2 * k, there),
            remote(shape_in.at[j, :, pl.ds(low, size)], shp.at[:, pl.ds(at, size)], 21 + k, there),
        ]

    def to_left(k, j):
        size, at = ((4, 14), (2, 18))[k]
        s_size, s_at = ((4, 15), (3, 19))[k]
        there = 2 * (chip - 1) + j
        return [
            remote(sensor_in.at[j, pl.ds(0, s_size)], sen.at[pl.ds(s_at, s_size)], 7 + 2 * k, there),
            remote(target_in.at[j, :, pl.ds(0, size)], g.at[:, pl.ds(at, size)], 8 + 2 * k, there),
            remote(shape_in.at[j, :, pl.ds(0, size)], shp.at[:, pl.ds(at, size)], 23 + k, there),
        ]

    first_round = []
    for near in (True, False):
        for make, there, k in ((to_right, has_right, 1 if near else 0), (to_left, has_left, 0 if near else 1)):
            pairs = [make(k, j) for j in range(2)]
            first_round.append(([[c[i] for c in pairs] for i in range(3)], jnp.logical_and(there, core == k)))
    other = 1 - core
    swap = [
        remote(sensor_in.at[other], sen.at[pl.ds(7 + 4 * core, 4)], 0, sibling),
        remote(target_in.at[other], g.at[:, pl.ds(6 + 4 * core, 4)], 1, sibling),
        remote(shape_in.at[other], shp.at[:, pl.ds(6 + 4 * core, 4)], 2, sibling),
    ]
    def send_first(items):
        for copies, there in items:
            @pl.when(there)
            def _(copies=copies):
                for copy in copies[0] + copies[1]:
                    copy.start()

    send_first(first_round[:2])
    for copy in swap[:2]:
        copy.start()
    send_first(first_round[2:])
    swap[2].start()
    for copies, there in first_round:
        @pl.when(there)
        def _(copies=copies):
            for copy in copies[2]:
                copy.start()

    tell(known_sem.at[0], beside)

    @pl.when(jnp.logical_not(has_left))
    def _():
        g[:, 0:6] = jnp.zeros((5, 6, 8, 128), F32)
        sen[0:7] = jnp.zeros((7, 8, 128), F32)
        halo[:, 0:6] = jnp.zeros((5, 6, 8, 128), F32)
        rp1[3:7] = jnp.zeros((4, 8, 128), F32)
        rp2[:, 0:3] = jnp.zeros((2, 3, 8, 128), F32)
        rc[0] = jnp.zeros(rc.shape[1:], F32)

    @pl.when(jnp.logical_not(has_right))
    def _():
        g[:, 14:20] = jnp.zeros((5, 6, 8, 128), F32)
        sen[15:22] = jnp.zeros((7, 8, 128), F32)
        halo[:, 6:12] = jnp.zeros((5, 6, 8, 128), F32)
        rp1[11:15] = jnp.zeros((4, 8, 128), F32)
        rp2[:, 7:10] = jnp.zeros((2, 3, 8, 128), F32)
        rc[2] = jnp.zeros(rc.shape[1:], F32)

    @pl.when(jnp.logical_not(has_left2))
    def _():
        rp1[0:3] = jnp.zeros((3, 8, 128), F32)

    @pl.when(jnp.logical_not(has_right2))
    def _():
        rp1[15:18] = jnp.zeros((3, 8, 128), F32)

    for copy in small:
        copy.wait()
    for d in range(3):
        for u in range(5):
            for v in range(5):
                jac[d * 25 + u * 5 + v] = jnp.full((8, 128), 0.5 * jac_in[d, u, core, v], F32)
    shift = jnp.full((8, 128), shift_in[core], F32)
    inverse = 1.0 / (shift * 32.0 + 48.0)

    from_left, from_right = ([make(k, 0) for k in range(2)] for make in (to_right, to_left))

    def arrive_first(i, copies, there):
        @pl.when(there)
        def _():
            for copy in copies:
                copy[i].wait_recv()

    mine[0].wait()
    swap[0].wait_recv()
    arrive_first(0, from_left, has_left)

    s, z = sublanes((1, 8, 128)), lanes((1, 8, 128))

    def coefficients(k, carry):
        i = 4 * k
        block = sen[pl.ds(i, 6)]
        near = block[1:5]
        x_plus, x_minus = (near + block[2:]) * 0.25, (near + block[:4]) * 0.25
        y_plus = (near + jnp.where(s < 7, up(near, 1), 0.0)) * 0.25
        y_minus = (near + jnp.where(s >= 1, down(near, 1), 0.0)) * 0.25
        z_plus = (near + jnp.where(z < 127, ahead(near, 1), 0.0)) * 0.25
        z_minus = (near + jnp.where(z >= 1, behind(near, 1), 0.0)) * 0.25
        total = shift[None] + ((x_plus + x_minus) + (y_plus + y_minus) + (z_plus + z_minus)) + 18.0 * EPS
        cpx[pl.ds(i + 1, 4)] = x_plus + 4.0 * EPS
        cyz[0, pl.ds(i, 4)] = jnp.where(s < 7, y_plus + 4.0 * EPS, 0.0)
        cyz[1, pl.ds(i, 4)] = jnp.where(s >= 1, y_minus + 4.0 * EPS, 0.0)
        cyz[2, pl.ds(i, 4)] = jnp.where(z < 127, z_plus + 4.0 * EPS, 0.0)
        cyz[3, pl.ds(i, 4)] = jnp.where(z >= 1, z_minus + 4.0 * EPS, 0.0)
        at = i + lax.broadcasted_iota(jnp.int32, total.shape, 0)
        inside = jnp.logical_and(at >= low_layer, at < high_layer)
        diag[pl.ds(i, 4)] = total
        w[pl.ds(i, 4)] = jnp.where(inside, RELAX / total, 0.0)
        return carry

    low_layer, high_layer = jnp.where(has_left, 0, 6), jnp.where(has_right, 20, 14)
    cpx[0:1] = (sen[0:1] + sen[1:2]) * 0.25 + 4.0 * EPS
    lax.fori_loop(0, 3, coefficients, 0)

    right, left = space + 2, space - 2

    def start(copies):
        for copy, there in copies:
            pl.when(there)(copy.start)

    def arrive(copies, theres):
        for (copy, _), there in zip(copies, theres):
            pl.when(there)(copy.wait_recv)

    def sent(copies):
        for copy, there in copies:
            pl.when(there)(copy.wait_send)

    def begin(k, carry):
        i = 4 * k
        weight = w[pl.ds(i, 4)]
        for v in range(5):
            b0[v, pl.ds(i + 2, 4)] = weight * g[v, pl.ds(i, 4)]
        return carry

    def sweep(src, dst, low, n, times, stride=None):
        part = 2

        def body(i, carry):
            results = []
            for k in range(n // part):
                at = low + i * (stride or n) + k * part
                center, out = off_diagonal(src, at, part, jac, cpx, cyz)
                weight = w[pl.ds(at - 2, part)]
                results.append([
                    (1.0 - RELAX) * center[v] + weight * (g[v, pl.ds(at - 2, part)] + out[v]) for v in range(5)
                ])
            for k, values in enumerate(results):
                for v in range(5):
                    dst[v, pl.ds(low + i * (stride or n) + k * part, part)] = values[v]
            return carry

        lax.fori_loop(0, times, body, 0)

    def restrict(src):
        def body(i, carry):
            at = 8 + i * 4
            center, out = off_diagonal(src, at, 4, jac, cpx, cyz)
            d = diag[pl.ds(at - 2, 4)]
            for v in range(5):
                r = g[v, pl.ds(at - 2, 4)] + out[v] - d * center[v]
                rs[v, pl.ds(2 * i, 1)] = r[0:1] + r[1:2]
                rs[v, pl.ds(2 * i + 1, 1)] = r[2:3] + r[3:4]
            return carry

        lax.fori_loop(0, 2, body, 0)
        return pack([rs[v] for v in range(5)])

    mine[1].wait()
    swap[1].wait_recv()
    arrive_first(1, from_left, has_left)
    lax.fori_loop(0, 3, begin, 0)
    sweep(b0, b1, 4, 8, 1)
    sweep(b1, b2, 6, 4, 1)
    early_halo = [(remote(b2.at[:, pl.ds(8, 2)], halo.at[:, pl.ds(0, 2)], 29, right), has_right)]
    start(early_halo)
    arrive_first(0, from_right, has_right)
    lax.fori_loop(3, 5, coefficients, 0)
    arrive_first(1, from_right, has_right)
    lax.fori_loop(3, 5, begin, 0)
    sweep(b0, b1, 12, 8, 1)
    sweep(b1, b2, 10, 8, 1)
    pl.semaphore_wait(known_sem.at[0], n_beside)
    tell(known_sem.at[1], [(space, preceding, None)])
    near_halos = [
        (remote(b2.at[:, pl.ds(12, 2)], halo.at[:, pl.ds(4, 2)], 11, right), has_right),
        (remote(b2.at[:, pl.ds(10, 2)], halo.at[:, pl.ds(6, 2)], 12, left), has_left),
    ]
    far_halos = [
        (remote(b2.at[:, pl.ds(10, 2)], halo.at[:, pl.ds(2, 2)], 19, right), has_right),
        (remote(b2.at[:, pl.ds(12, 4)], halo.at[:, pl.ds(8, 4)], 20, left), has_left),
    ]
    start(near_halos)
    rp1[7:11] = restrict(b2)
    boxes = [
        (remote(rp1.at[pl.ds(7, 4)], rp1.at[pl.ds(3, 4)], 15, right), has_right),
        (remote(rp1.at[pl.ds(7, 4)], rp1.at[pl.ds(11, 4)], 16, left), has_left),
        (remote(rp1.at[pl.ds(8, 3)], rp1.at[pl.ds(0, 3)], 13, space + 4), has_right2),
        (remote(rp1.at[pl.ds(7, 3)], rp1.at[pl.ds(15, 3)], 14, space - 4), has_left2),
    ]
    start(boxes)
    start(far_halos)
    arrive(boxes, (has_left, has_right, has_left2, has_right2))
    last_box = 4 * chips - 1
    c = coarse_solve(rp1[...], 4 * chip - 7, last_box, inverse[None])
    at = 4 * chip - 4 + lax.broadcasted_iota(jnp.int32, c.shape, 0)
    fixes = unpack(jnp.where(jnp.logical_and(at >= 0, at <= last_box), c, 0.0))

    def correct(old, low, high):
        for v in range(5):
            for i in range(low, high):
                b1[v, i] = old(v, i) + fixes[v][i // 2]

    arrive(near_halos, (has_left, has_right))
    correct(lambda v, i: halo[v, i], 4, 6)
    correct(lambda v, i: b2[v, i], 6, 18)
    correct(lambda v, i: halo[v, i - 12], 18, 20)
    sweep(b1, b0, 6, 6, 2)
    sweep(b0, b1, 8, 8, 1)
    arrive(early_halo + far_halos, (has_left, has_left, has_right))
    correct(lambda v, i: halo[v, i], 0, 4)
    correct(lambda v, i: halo[v, i - 12], 20, 24)
    sweep(b1, b0, 2, 4, 2, 16)
    sweep(b0, b1, 4, 4, 2, 12)
    sweep(b1, b0, 6, 6, 2)
    over = remote(b0.at[:, pl.ds(8 + 4 * other, 4)], sib, 25, sibling)
    over.start()
    rp2[core, 3:7] = restrict(b0)

    def boxes_beside(c_at, j):
        return [
            (remote(rp2.at[c_at, pl.ds(4, 3)], rp2.at[c_at, pl.ds(0, 3)], 17 + 9 * c_at, right - core + j), has_right),
            (remote(rp2.at[c_at, pl.ds(3, 3)], rp2.at[c_at, pl.ds(7, 3)], 18 + 9 * c_at, left - core + j), has_left),
        ]

    boxes2 = boxes_beside(core, 0) + boxes_beside(core, 1)

    weight = jnp.full((8, 128), weight_in[core], F32)
    mine[2].wait()
    swap[2].wait_recv()
    arrive_first(2, from_left, has_left)
    arrive_first(2, from_right, has_right)
    fixes = unpack(coarse_spread(rp2[core, 3:7], 4 * chip, last_box, inverse[None]))
    parts = []
    for i in range(20):
        total = None
        for v in range(5):
            value = fixes[v][i // 2]
            if 6 <= i < 14:
                value = value + b0[v, 2 + i]
            term = value * shp[v, i]
            total = term if total is None else total + term
        parts.append(weight * total)
    s2 = sublanes((8, 128))
    for d in range(3):
        for j in range(2):
            for c_to in range(n_cond):
                gathered = jnp.zeros((8, 128), F32)
                for i in range(4):
                    at = 8 * d - 2 + 4 * j + i
                    turn = (rows * i - rows * c_to) % 8
                    moved = jnp.zeros((8, 128), F32)
                    if 0 <= at < 20:
                        moved = parts[at] if turn == 0 else down(parts[at], turn)
                    gathered = jnp.where(s2 >= rows * i, moved, gathered) if i else moved
                cs[d, j * n_cond + c_to] = gathered
    me = 2 * cond + core

    def share(d, j, c_to):
        return pltpu.make_async_remote_copy(
            src_ref=cs.at[d, j * n_cond + c_to], dst_ref=rc.at[2 - d, me], send_sem=share_sem.at[d], recv_sem=share_sem.at[5 - d],
            device_id={"space": 2 * (chip + d - 1) + j, "cond": c_to},
        )

    def shared(d, slots):
        return pltpu.make_async_remote_copy(
            src_ref=cs.at[d, pl.ds(0, slots)], dst_ref=rc.at[d, pl.ds(0, slots)], send_sem=share_sem.at[d], recv_sem=share_sem.at[3 + d],
            device_id={"space": sibling, "cond": cond},
        )

    pl.semaphore_wait(known_sem.at[1], 1)
    outer = ((0, has_left), (2, has_right))
    for dz in (2, 1, 3, 0):
        for d, there in outer:
            @pl.when(there)
            def _(d=d, dz=dz):
                for j in range(2):
                    share(d, j, lax.rem(cond + dz, n_cond)).start()
    for s_to, c_to in reversed(ring[1:]):
        share(1, lax.rem(s_to, 2), c_to).start()
    rc[1, me] = cs[1, core * n_cond + cond]

    start(boxes2)
    boxes_over = remote(rp2.at[core, pl.ds(3, 4)], rp2.at[core, pl.ds(3, 4)], 28, sibling)
    boxes_over.start()

    arrive(boxes_beside(0, 0) + boxes_beside(1, 0), (has_left, has_right) * 2)
    boxes_over.wait_recv()
    over.wait_recv()
    for c_at, old in ((core, lambda v: b0[v, pl.ds(8 + 4 * core, 4)]), (other, lambda v: sib[v])):
        inv = 1.0 / (jnp.full((1, 8, 128), shift_in[c_at], F32) * 32.0 + 48.0)
        c = coarse_solve(rp2[c_at, pl.ds(2 * core, 8)], 4 * chip - 3 + 2 * core, last_box, inv)
        fixes = unpack(c)
        for v in range(5):
            value = old(v)
            for i in range(4):
                adjoint_out[c_at, v, i] = value[i] + fixes[v][i // 2]

    for d, there in outer:
        pl.when(there)(shared(d, 2 * n_cond).wait_recv)
    shared(1, 2 * n_cond - 1).wait_recv()
    total = None
    for d in range(3):
        for i in range(2 * n_cond):
            total = rc[d, i] if total is None else total + rc[d, i]
    for i in range(4):
        sens_out[i] = total[rows * i : rows * (i + 1)]
    over.wait_send()
    boxes_over.wait_send()
    for d, there in outer:
        pl.when(there)(shared(d, 2 * n_cond).wait_send)
    shared(1, 2 * n_cond - 1).wait_send()
    for copy in swap:
        copy.wait_send()
    for copies, there in first_round:
        @pl.when(there)
        def _(copies=copies):
            for copy in copies[0] + copies[1] + copies[2]:
                copy.wait_send()
    sent(early_halo + near_halos + far_halos + boxes + boxes2)


def settle(adjoint, sens, adjoint_out, sens_out, sem):
    copies = [pltpu.make_async_copy(adjoint, adjoint_out, sem.at[0]), pltpu.make_async_copy(sens, sens_out, sem.at[1])]
    for copy in copies:
        copy.start()
    for copy in copies:
        copy.wait()


def solution(mesh):
    n_cond, n_space = mesh.shape["cond"], mesh.shape["space"]
    rows = 8 // n_cond

    def local(target, shape, jac, sensor, shift, weight, agglomeration, links):
        vmem = lambda *shape: pltpu.VMEM((*shape, 8, 128), F32)
        hbm = pl.BlockSpec(memory_space=pltpu.HBM)
        stay = lambda x: pltpu.with_memory_space_constraint(x, pltpu.HBM)
        operands = (target, shape, jnp.transpose(jac, (1, 2, 0, 3)), sensor, shift, weight)
        adjoint, sens = pl.pallas_call(
            functools.partial(kernel, n_cond, n_space),
            out_shape=(
                pltpu.VMEM(target.shape, F32),
                pltpu.VMEM((4, rows, 128), F32),
            ),
            in_specs=[hbm] * 6,
            out_specs=(pl.BlockSpec(memory_space=pltpu.VMEM),) * 2,
            scratch_shapes=[
                pltpu.SMEM((3, 5, 2, 5), F32), pltpu.SMEM((2,), F32), pltpu.SMEM((2,), F32),
                vmem(5, 20), vmem(22), vmem(5, 20),
                vmem(21), vmem(4, 20), vmem(20), vmem(20), vmem(75),
                vmem(5, 24), vmem(5, 24), vmem(5, 24), vmem(5, 12), vmem(5, 4),
                vmem(18), vmem(2, 10), vmem(5, 4), vmem(3, 2 * n_cond), vmem(3, 2 * n_cond),
                pltpu.SemaphoreType.DMA((6,)),
                pltpu.SemaphoreType.DMA((64,)),
                pltpu.SemaphoreType.DMA((30,)),
                pltpu.SemaphoreType.DMA((6,)),
                pltpu.SemaphoreType.REGULAR((2,)),
            ],
            compiler_params=pltpu.CompilerParams(
                collective_id=0, has_side_effects=True, vmem_limit_bytes=48 * 2**20
            ),
        )(*map(stay, operands))
        return pl.pallas_call(
            settle,
            out_shape=(pltpu.HBM(adjoint.shape, F32), pltpu.HBM(sens.shape, F32)),
            in_specs=[pl.BlockSpec(memory_space=pltpu.VMEM)] * 2,
            out_specs=(hbm, hbm),
            scratch_shapes=[pltpu.SemaphoreType.DMA((2,))],
        )(*(pltpu.with_memory_space_constraint(x, pltpu.VMEM) for x in (adjoint, sens)))

    in_specs = (
        P("cond", None, "space", None, None),
        P("cond", None, "space", None, None),
        P("cond", None, None, None),
        P("cond", "space", None, None),
        P("cond"),
        P("cond"),
        P("space", None, None),
        P(None, "space"),
    )
    out_specs = (P("cond", None, "space", None, None), P("space", "cond", None))
    return jax.shard_map(local, mesh=mesh, in_specs=in_specs, out_specs=out_specs, check_vma=False)
```

```python
import functools

import jax
import jax.numpy as jnp
from jax import lax
from jax.experimental import pallas as pl
from jax.experimental.pallas import tpu as pltpu
from jax.sharding import PartitionSpec as P

RELAX = 0.7
EPS = 1.0 / 32.0
F32 = jnp.float32


def sublanes(shape):
    return lax.broadcasted_iota(jnp.int32, shape, len(shape) - 2)


def lanes(shape):
    return lax.broadcasted_iota(jnp.int32, shape, len(shape) - 1)


def up(a, n):
    return pltpu.roll(a, 8 - n, a.ndim - 2)


def down(a, n):
    return pltpu.roll(a, n, a.ndim - 2)


def ahead(a, n):
    return pltpu.roll(a, 128 - n, a.ndim - 1)


def behind(a, n):
    return pltpu.roll(a, n, a.ndim - 1)


def pack(v):
    s, z = sublanes(v[0].shape), lanes(v[0].shape)
    even, low = s % 2 == 0, s % 4 < 2
    zeven, zlow = z % 2 == 0, z % 4 < 2

    def pair(a, b):
        return jnp.where(even, a, b) + jnp.where(even, up(a, 1), down(b, 1))

    def quad(a, b):
        return jnp.where(low, a, b) + jnp.where(low, up(a, 2), down(b, 2))

    four = quad(pair(v[0], v[1]), pair(v[2], v[3]))
    last = pair(v[4], v[4])
    last = quad(last, last)
    both = jnp.where(zeven, four, last) + jnp.where(zeven, ahead(four, 1), behind(last, 1))
    return both + jnp.where(zlow, ahead(both, 2), behind(both, 2))


def unpack(c):
    s, z = sublanes(c.shape), lanes(c.shape)
    even, low, zeven = s % 2 == 0, s % 4 < 2, z % 2 == 0
    four = jnp.where(zeven, c, behind(c, 1))
    last = jnp.where(zeven, ahead(c, 1), c)
    p02 = jnp.where(even, four, down(four, 1))
    p13 = jnp.where(even, up(four, 1), four)
    return (
        jnp.where(low, p02, down(p02, 2)),
        jnp.where(low, p13, down(p13, 2)),
        jnp.where(low, up(p02, 2), p02),
        jnp.where(low, up(p13, 2), p13),
        last,
    )


def neighbours(c, first, last_box):
    own = c[1:-1]
    at = first + lax.broadcasted_iota(jnp.int32, own.shape, 0)
    z = lanes(own.shape)
    total = jnp.where(at == 0, own, c[:-2]) + jnp.where(at == last_box, own, c[2:])
    total = total + (own + up(own, 4))
    return total + jnp.where(z < 4, own, behind(own, 4)) + jnp.where(z >= 124, own, ahead(own, 4))


def coarse_solve(res, first, last_box, inverse):
    scaled = res * inverse
    c = scaled
    for sweep in range(1, 4):
        c = scaled[sweep:-sweep] + 8.0 * inverse * neighbours(c, first + sweep, last_box)
    return c


def coarse_spread(res, first, last_box, inverse):
    none = jnp.zeros((1, 8, 128), F32)
    scaled = res * inverse
    c = scaled
    for sweep in range(1, 4):
        scaled = jnp.concatenate([none, scaled, none])
        c = scaled + 8.0 * inverse * neighbours(jnp.concatenate([none, none, c, none, none]), first - sweep, last_box)
    return c


def off_diagonal(field, at, n, jac, cpx, cyz):
    s, z = sublanes((1, 8, 128)), lanes((1, 8, 128))
    y_not_last, y_not_first = jnp.where(s < 7, 1.0, 0.0), jnp.where(s >= 1, 1.0, 0.0)
    z_not_last, z_not_first = jnp.where(z < 127, 1.0, 0.0), jnp.where(z >= 1, 1.0, 0.0)
    y_far_up, y_far_down = jnp.where(s < 6, -EPS, 0.0), jnp.where(s >= 2, -EPS, 0.0)
    z_far_up, z_far_down = jnp.where(z < 126, -EPS, 0.0), jnp.where(z >= 2, -EPS, 0.0)
    cx = cpx[pl.ds(at - 2, n + 1)]
    cy_plus, cy_minus, cz_plus, cz_minus = (cyz[i, pl.ds(at - 2, n)] for i in range(4))
    center, out = [], [None] * 5

    def add(v, term):
        out[v] = term if out[v] is None else out[v] + term

    for u in range(5):
        block = field[u, pl.ds(at - 2, n + 4)]
        a, plus, minus = block[2:-2], block[3:-1], block[1:-3]
        center.append(a)
        total = cx[1:] * plus
        total = total + cx[:-1] * minus
        total = total - EPS * (block[4:] + block[:-4])
        dx = plus - minus
        plus, minus = up(a, 1), down(a, 1)
        total = total + cy_plus * plus
        total = total + cy_minus * minus
        total = total + y_far_up * up(a, 2)
        total = total + y_far_down * down(a, 2)
        dy = y_not_last * plus - y_not_first * minus
        plus, minus = ahead(a, 1), behind(a, 1)
        total = total + cz_plus * plus
        total = total + cz_minus * minus
        total = total + z_far_up * ahead(a, 2)
        total = total + z_far_down * behind(a, 2)
        dz = z_not_last * plus - z_not_first * minus
        add(u, total)
        for d, diff in enumerate((dx, dy, dz)):
            for v in range(5):
                add(v, jac[d * 25 + u * 5 + v] * diff)
    return center, out


def kernel(
    n_cond, n_space, target_in, shape_in, jac_hbm, sensor_in, shift_hbm, weight_hbm, adjoint_out, sens_out,
    jac_in, shift_in, weight_in, sen_stage, g_stage, g, sen, shp, cpx, cyz, w, diag, jac, b0, b1, b2, halo, rs, rp1, rp2, sib, cs, rc, local_sem, send_sem, recv_sem, share_sem, known_sem,
):
    space, cond = lax.axis_index("space"), lax.axis_index("cond")
    chip, core = space // 2, space % 2
    chips = n_space // 2
    has_left, has_right = chip > 0, chip < chips - 1
    has_left2, has_right2 = chip > 1, chip < chips - 2
    rows = 8 // n_cond

    ring = [(2 * chip + (core + j) % 2, lax.rem(cond + dz, n_cond)) for dz in range(n_cond) for j in range(2)]
    sibling = 2 * chip + 1 - core
    following, preceding = lax.rem(cond + 1, n_cond), lax.rem(cond + n_cond - 1, n_cond)
    beside = [(2 * (chip + near) + j, cond, there) for near, there in ((-1, has_left), (1, has_right)) for j in range(2)]
    beside += [(sibling, cond, None), (space, following, None), (space, preceding, None)]
    n_beside = 3 + 2 * (has_left.astype(jnp.int32) + has_right.astype(jnp.int32))

    def tell(semaphore, peers):
        for s, c, there in peers:
            def one(s=s, c=c):
                pl.semaphore_signal(semaphore, inc=1, device_id={"space": s, "cond": c})
            one() if there is None else pl.when(there)(one)

    barrier = pltpu.get_barrier_semaphore()
    tell(barrier, beside)

    count = iter(range(1000))
    sends = []

    def remote(src, dst, recv, s, c=cond):
        return pltpu.make_async_remote_copy(
            src_ref=src, dst_ref=dst, send_sem=send_sem.at[next(count)], recv_sem=recv_sem.at[recv],
            device_id={"space": s, "cond": c},
        )

    mine = [
        pltpu.make_async_copy(sensor_in.at[core], sen.at[pl.ds(7 + 4 * core, 4)], local_sem.at[0]),
        pltpu.make_async_copy(target_in.at[core], g.at[:, pl.ds(6 + 4 * core, 4)], local_sem.at[1]),
        pltpu.make_async_copy(shape_in.at[core], shp.at[:, pl.ds(6 + 4 * core, 4)], local_sem.at[2]),
    ]
    small = [
        pltpu.make_async_copy(jac_hbm, jac_in, local_sem.at[3]),
        pltpu.make_async_copy(shift_hbm, shift_in, local_sem.at[4]),
        pltpu.make_async_copy(weight_hbm, weight_in, local_sem.at[5]),
    ]
    stage = [
        pltpu.make_async_copy(sensor_in, sen_stage, local_sem.at[6]),
        pltpu.make_async_copy(target_in, g_stage, local_sem.at[7]),
    ]
    for copy in stage + small + mine:
        copy.start()

    pl.semaphore_wait(barrier, n_beside)
    for copy in stage:
        copy.wait()

    def to_right(k, j):
        low, size, at = ((2, 2, 0), (0, 4, 2))[k]
        s_low, s_size, s_at = ((1, 3, 0), (0, 4, 3))[k]
        there = 2 * (chip + 1) + j
        return [
            remote(sen_stage.at[j, pl.ds(s_low, s_size)], sen.at[pl.ds(s_at, s_size)], 3 + 2 * k, there),
            remote(g_stage.at[j, :, pl.ds(low, size)], g.at[:, pl.ds(at, size)], 4 + 2 * k, there),
            remote(shape_in.at[j, :, pl.ds(low, size)], shp.at[:, pl.ds(at, size)], 21 + k, there),
        ]

    def to_left(k, j):
        size, at = ((4, 14), (2, 18))[k]
        s_size, s_at = ((4, 15), (3, 19))[k]
        there = 2 * (chip - 1) + j
        return [
            remote(sen_stage.at[j, pl.ds(0, s_size)], sen.at[pl.ds(s_at, s_size)], 7 + 2 * k, there),
            remote(g_stage.at[j, :, pl.ds(0, size)], g.at[:, pl.ds(at, size)], 8 + 2 * k, there),
            remote(shape_in.at[j, :, pl.ds(0, size)], shp.at[:, pl.ds(at, size)], 23 + k, there),
        ]

    first_round = []
    for near in (True, False):
        for make, there, k in ((to_right, has_right, 1 if near else 0), (to_left, has_left, 0 if near else 1)):
            pairs = [make(k, j) for j in range(2)]
            first_round.append(([[c[i] for c in pairs] for i in range(3)], jnp.logical_and(there, core == k)))
    other = 1 - core
    swap = [
        remote(sen_stage.at[other], sen.at[pl.ds(7 + 4 * core, 4)], 0, sibling),
        remote(g_stage.at[other], g.at[:, pl.ds(6 + 4 * core, 4)], 1, sibling),
        remote(shape_in.at[other], shp.at[:, pl.ds(6 + 4 * core, 4)], 2, sibling),
    ]
    def send_first(items):
        for copies, there in items:
            @pl.when(there)
            def _(copies=copies):
                for copy in copies[0] + copies[1]:
                    copy.start()

    send_first(first_round[:2])
    for copy in swap[:2]:
        copy.start()
    send_first(first_round[2:])
    swap[2].start()
    for copies, there in first_round:
        @pl.when(there)
        def _(copies=copies):
            for copy in copies[2]:
                copy.start()

    tell(known_sem.at[0], beside)

    @pl.when(jnp.logical_not(has_left))
    def _():
        g[:, 0:6] = jnp.zeros((5, 6, 8, 128), F32)
        sen[0:7] = jnp.zeros((7, 8, 128), F32)
        halo[:, 0:6] = jnp.zeros((5, 6, 8, 128), F32)
        rp1[3:7] = jnp.zeros((4, 8, 128), F32)
        rp2[:, 0:3] = jnp.zeros((2, 3, 8, 128), F32)
        rc[0] = jnp.zeros(rc.shape[1:], F32)

    @pl.when(jnp.logical_not(has_right))
    def _():
        g[:, 14:20] = jnp.zeros((5, 6, 8, 128), F32)
        sen[15:22] = jnp.zeros((7, 8, 128), F32)
        halo[:, 6:12] = jnp.zeros((5, 6, 8, 128), F32)
        rp1[11:15] = jnp.zeros((4, 8, 128), F32)
        rp2[:, 7:10] = jnp.zeros((2, 3, 8, 128), F32)
        rc[2] = jnp.zeros(rc.shape[1:], F32)

    @pl.when(jnp.logical_not(has_left2))
    def _():
        rp1[0:3] = jnp.zeros((3, 8, 128), F32)

    @pl.when(jnp.logical_not(has_right2))
    def _():
        rp1[15:18] = jnp.zeros((3, 8, 128), F32)

    for copy in small:
        copy.wait()
    for d in range(3):
        for u in range(5):
            for v in range(5):
                jac[d * 25 + u * 5 + v] = jnp.full((8, 128), 0.5 * jac_in[d, u, core, v], F32)
    shift = jnp.full((8, 128), shift_in[core], F32)
    inverse = 1.0 / (shift * 32.0 + 48.0)

    from_left, from_right = ([make(k, 0) for k in range(2)] for make in (to_right, to_left))

    def arrive_first(i, copies, there):
        @pl.when(there)
        def _():
            for copy in copies:
                copy[i].wait_recv()

    mine[0].wait()
    swap[0].wait_recv()
    arrive_first(0, from_left, has_left)

    s, z = sublanes((1, 8, 128)), lanes((1, 8, 128))

    def coefficients(k, carry):
        i = 4 * k
        block = sen[pl.ds(i, 6)]
        near = block[1:5]
        x_plus, x_minus = (near + block[2:]) * 0.25, (near + block[:4]) * 0.25
        y_plus = (near + jnp.where(s < 7, up(near, 1), 0.0)) * 0.25
        y_minus = (near + jnp.where(s >= 1, down(near, 1), 0.0)) * 0.25
        z_plus = (near + jnp.where(z < 127, ahead(near, 1), 0.0)) * 0.25
        z_minus = (near + jnp.where(z >= 1, behind(near, 1), 0.0)) * 0.25
        total = shift[None] + ((x_plus + x_minus) + (y_plus + y_minus) + (z_plus + z_minus)) + 18.0 * EPS
        cpx[pl.ds(i + 1, 4)] = x_plus + 4.0 * EPS
        cyz[0, pl.ds(i, 4)] = jnp.where(s < 7, y_plus + 4.0 * EPS, 0.0)
        cyz[1, pl.ds(i, 4)] = jnp.where(s >= 1, y_minus + 4.0 * EPS, 0.0)
        cyz[2, pl.ds(i, 4)] = jnp.where(z < 127, z_plus + 4.0 * EPS, 0.0)
        cyz[3, pl.ds(i, 4)] = jnp.where(z >= 1, z_minus + 4.0 * EPS, 0.0)
        at = i + lax.broadcasted_iota(jnp.int32, total.shape, 0)
        inside = jnp.logical_and(at >= low_layer, at < high_layer)
        diag[pl.ds(i, 4)] = total
        w[pl.ds(i, 4)] = jnp.where(inside, RELAX / total, 0.0)
        return carry

    low_layer, high_layer = jnp.where(has_left, 0, 6), jnp.where(has_right, 20, 14)
    cpx[0:1] = (sen[0:1] + sen[1:2]) * 0.25 + 4.0 * EPS
    lax.fori_loop(0, 3, coefficients, 0)

    right, left = space + 2, space - 2

    def start(copies):
        for copy, there in copies:
            pl.when(there)(copy.start)

    def arrive(copies, theres):
        for (copy, _), there in zip(copies, theres):
            pl.when(there)(copy.wait_recv)

    def sent(copies):
        for copy, there in copies:
            pl.when(there)(copy.wait_send)

    def begin(k, carry):
        i = 4 * k
        weight = w[pl.ds(i, 4)]
        for v in range(5):
            b0[v, pl.ds(i + 2, 4)] = weight * g[v, pl.ds(i, 4)]
        return carry

    def sweep(src, dst, low, n, times, stride=None):
        part = 2

        def body(i, carry):
            results = []
            for k in range(n // part):
                at = low + i * (stride or n) + k * part
                center, out = off_diagonal(src, at, part, jac, cpx, cyz)
                weight = w[pl.ds(at - 2, part)]
                results.append([
                    (1.0 - RELAX) * center[v] + weight * (g[v, pl.ds(at - 2, part)] + out[v]) for v in range(5)
                ])
            for k, values in enumerate(results):
                for v in range(5):
                    dst[v, pl.ds(low + i * (stride or n) + k * part, part)] = values[v]
            return carry

        lax.fori_loop(0, times, body, 0)

    def restrict(src):
        def body(i, carry):
            at = 8 + i * 4
            center, out = off_diagonal(src, at, 4, jac, cpx, cyz)
            d = diag[pl.ds(at - 2, 4)]
            for v in range(5):
                r = g[v, pl.ds(at - 2, 4)] + out[v] - d * center[v]
                rs[v, pl.ds(2 * i, 1)] = r[0:1] + r[1:2]
                rs[v, pl.ds(2 * i + 1, 1)] = r[2:3] + r[3:4]
            return carry

        lax.fori_loop(0, 2, body, 0)
        return pack([rs[v] for v in range(5)])

    mine[1].wait()
    swap[1].wait_recv()
    arrive_first(1, from_left, has_left)
    lax.fori_loop(0, 3, begin, 0)
    sweep(b0, b1, 4, 8, 1)
    sweep(b1, b2, 6, 4, 1)
    early_halo = [(remote(b2.at[:, pl.ds(8, 2)], halo.at[:, pl.ds(0, 2)], 29, right), has_right)]
    start(early_halo)
    arrive_first(0, from_right, has_right)
    lax.fori_loop(3, 5, coefficients, 0)
    arrive_first(1, from_right, has_right)
    lax.fori_loop(3, 5, begin, 0)
    sweep(b0, b1, 12, 8, 1)
    sweep(b1, b2, 10, 8, 1)
    pl.semaphore_wait(known_sem.at[0], n_beside)
    tell(known_sem.at[1], [(space, preceding, None)])
    near_halos = [
        (remote(b2.at[:, pl.ds(12, 2)], halo.at[:, pl.ds(4, 2)], 11, right), has_right),
        (remote(b2.at[:, pl.ds(10, 2)], halo.at[:, pl.ds(6, 2)], 12, left), has_left),
    ]
    far_halos = [
        (remote(b2.at[:, pl.ds(10, 2)], halo.at[:, pl.ds(2, 2)], 19, right), has_right),
        (remote(b2.at[:, pl.ds(12, 4)], halo.at[:, pl.ds(8, 4)], 20, left), has_left),
    ]
    start(near_halos)
    rp1[7:11] = restrict(b2)
    boxes = [
        (remote(rp1.at[pl.ds(7, 4)], rp1.at[pl.ds(3, 4)], 15, right), has_right),
        (remote(rp1.at[pl.ds(7, 4)], rp1.at[pl.ds(11, 4)], 16, left), has_left),
        (remote(rp1.at[pl.ds(8, 3)], rp1.at[pl.ds(0, 3)], 13, space + 4), has_right2),
        (remote(rp1.at[pl.ds(7, 3)], rp1.at[pl.ds(15, 3)], 14, space - 4), has_left2),
    ]
    start(boxes)
    start(far_halos)
    arrive(boxes, (has_left, has_right, has_left2, has_right2))
    last_box = 4 * chips - 1
    c = coarse_solve(rp1[...], 4 * chip - 7, last_box, inverse[None])
    at = 4 * chip - 4 + lax.broadcasted_iota(jnp.int32, c.shape, 0)
    fixes = unpack(jnp.where(jnp.logical_and(at >= 0, at <= last_box), c, 0.0))

    def correct(old, low, high):
        for v in range(5):
            for i in range(low, high):
                b1[v, i] = old(v, i) + fixes[v][i // 2]

    arrive(near_halos, (has_left, has_right))
    correct(lambda v, i: halo[v, i], 4, 6)
    correct(lambda v, i: b2[v, i], 6, 18)
    correct(lambda v, i: halo[v, i - 12], 18, 20)
    sweep(b1, b0, 6, 6, 2)
    sweep(b0, b1, 8, 8, 1)
    arrive(early_halo + far_halos, (has_left, has_left, has_right))
    correct(lambda v, i: halo[v, i], 0, 4)
    correct(lambda v, i: halo[v, i - 12], 20, 24)
    sweep(b1, b0, 2, 4, 2, 16)
    sweep(b0, b1, 4, 4, 2, 12)
    sweep(b1, b0, 6, 6, 2)
    over = remote(b0.at[:, pl.ds(8 + 4 * other, 4)], sib, 25, sibling)
    over.start()
    rp2[core, 3:7] = restrict(b0)

    def boxes_beside(c_at, j):
        return [
            (remote(rp2.at[c_at, pl.ds(4, 3)], rp2.at[c_at, pl.ds(0, 3)], 17 + 9 * c_at, right - core + j), has_right),
            (remote(rp2.at[c_at, pl.ds(3, 3)], rp2.at[c_at, pl.ds(7, 3)], 18 + 9 * c_at, left - core + j), has_left),
        ]

    boxes2 = boxes_beside(core, 0) + boxes_beside(core, 1)

    weight = jnp.full((8, 128), weight_in[core], F32)
    mine[2].wait()
    swap[2].wait_recv()
    arrive_first(2, from_left, has_left)
    arrive_first(2, from_right, has_right)
    fixes = unpack(coarse_spread(rp2[core, 3:7], 4 * chip, last_box, inverse[None]))
    parts = []
    for i in range(20):
        total = None
        for v in range(5):
            value = fixes[v][i // 2]
            if 6 <= i < 14:
                value = value + b0[v, 2 + i]
            term = value * shp[v, i]
            total = term if total is None else total + term
        parts.append(weight * total)
    s2 = sublanes((8, 128))
    for d in range(3):
        for j in range(2):
            for c_to in range(n_cond):
                gathered = jnp.zeros((8, 128), F32)
                for i in range(4):
                    at = 8 * d - 2 + 4 * j + i
                    turn = (rows * i - rows * c_to) % 8
                    moved = jnp.zeros((8, 128), F32)
                    if 0 <= at < 20:
                        moved = parts[at] if turn == 0 else down(parts[at], turn)
                    gathered = jnp.where(s2 >= rows * i, moved, gathered) if i else moved
                cs[d, j * n_cond + c_to] = gathered
    me = 2 * cond + core

    def share(d, j, c_to):
        return pltpu.make_async_remote_copy(
            src_ref=cs.at[d, j * n_cond + c_to], dst_ref=rc.at[2 - d, me], send_sem=share_sem.at[d], recv_sem=share_sem.at[5 - d],
            device_id={"space": 2 * (chip + d - 1) + j, "cond": c_to},
        )

    def shared(d, slots):
        return pltpu.make_async_remote_copy(
            src_ref=cs.at[d, pl.ds(0, slots)], dst_ref=rc.at[d, pl.ds(0, slots)], send_sem=share_sem.at[d], recv_sem=share_sem.at[3 + d],
            device_id={"space": sibling, "cond": cond},
        )

    pl.semaphore_wait(known_sem.at[1], 1)
    outer = ((0, has_left), (2, has_right))
    for dz in (2, 1, 3, 0):
        for d, there in outer:
            @pl.when(there)
            def _(d=d, dz=dz):
                for j in range(2):
                    share(d, j, lax.rem(cond + dz, n_cond)).start()
    for s_to, c_to in reversed(ring[1:]):
        share(1, lax.rem(s_to, 2), c_to).start()
    rc[1, me] = cs[1, core * n_cond + cond]

    start(boxes2)
    boxes_over = remote(rp2.at[core, pl.ds(3, 4)], rp2.at[core, pl.ds(3, 4)], 28, sibling)
    boxes_over.start()

    arrive(boxes_beside(0, 0) + boxes_beside(1, 0), (has_left, has_right) * 2)
    boxes_over.wait_recv()
    over.wait_recv()
    for c_at, old in ((core, lambda v: b0[v, pl.ds(8 + 4 * core, 4)]), (other, lambda v: sib[v])):
        inv = 1.0 / (jnp.full((1, 8, 128), shift_in[c_at], F32) * 32.0 + 48.0)
        c = coarse_solve(rp2[c_at, pl.ds(2 * core, 8)], 4 * chip - 3 + 2 * core, last_box, inv)
        fixes = unpack(c)
        for v in range(5):
            value = old(v)
            for i in range(4):
                adjoint_out[c_at, v, i] = value[i] + fixes[v][i // 2]

    over.wait_send()
    boxes_over.wait_send()
    for copy in swap:
        copy.wait_send()
    for copies, there in first_round:
        @pl.when(there)
        def _(copies=copies):
            for copy in copies[0] + copies[1] + copies[2]:
                copy.wait_send()
    sent(early_halo + near_halos + far_halos + boxes + boxes2)

    for d, there in outer:
        pl.when(there)(shared(d, 2 * n_cond).wait_recv)
    shared(1, 2 * n_cond - 1).wait_recv()
    total = None
    for d in range(3):
        for i in range(2 * n_cond):
            total = rc[d, i] if total is None else total + rc[d, i]
    for i in range(4):
        sens_out[i] = total[rows * i : rows * (i + 1)]
    for d, there in outer:
        pl.when(there)(shared(d, 2 * n_cond).wait_send)
    shared(1, 2 * n_cond - 1).wait_send()


def settle(adjoint, sens, adjoint_out, sens_out, sem):
    copies = [pltpu.make_async_copy(adjoint, adjoint_out, sem.at[0]), pltpu.make_async_copy(sens, sens_out, sem.at[1])]
    for copy in copies:
        copy.start()
    for copy in copies:
        copy.wait()


def solution(mesh):
    n_cond, n_space = mesh.shape["cond"], mesh.shape["space"]
    rows = 8 // n_cond

    def local(target, shape, jac, sensor, shift, weight, agglomeration, links):
        vmem = lambda *shape: pltpu.VMEM((*shape, 8, 128), F32)
        hbm = pl.BlockSpec(memory_space=pltpu.HBM)
        stay = lambda x: pltpu.with_memory_space_constraint(x, pltpu.HBM)
        operands = (target, shape, jnp.transpose(jac, (1, 2, 0, 3)), sensor, shift, weight)
        adjoint, sens = pl.pallas_call(
            functools.partial(kernel, n_cond, n_space),
            out_shape=(
                pltpu.VMEM(target.shape, F32),
                pltpu.VMEM((4, rows, 128), F32),
            ),
            in_specs=[hbm] * 6,
            out_specs=(pl.BlockSpec(memory_space=pltpu.VMEM),) * 2,
            scratch_shapes=[
                pltpu.SMEM((3, 5, 2, 5), F32), pltpu.SMEM((2,), F32), pltpu.SMEM((2,), F32),
                vmem(2, 4), vmem(2, 5, 4),
                vmem(5, 20), vmem(22), vmem(5, 20),
                vmem(21), vmem(4, 20), vmem(20), vmem(20), vmem(75),
                vmem(5, 24), vmem(5, 24), vmem(5, 24), vmem(5, 12), vmem(5, 4),
                vmem(18), vmem(2, 10), vmem(5, 4), vmem(3, 2 * n_cond), vmem(3, 2 * n_cond),
                pltpu.SemaphoreType.DMA((8,)),
                pltpu.SemaphoreType.DMA((64,)),
                pltpu.SemaphoreType.DMA((30,)),
                pltpu.SemaphoreType.DMA((6,)),
                pltpu.SemaphoreType.REGULAR((2,)),
            ],
            compiler_params=pltpu.CompilerParams(
                collective_id=0, has_side_effects=True, vmem_limit_bytes=48 * 2**20
            ),
        )(*map(stay, operands))
        return pl.pallas_call(
            settle,
            out_shape=(pltpu.HBM(adjoint.shape, F32), pltpu.HBM(sens.shape, F32)),
            in_specs=[pl.BlockSpec(memory_space=pltpu.VMEM)] * 2,
            out_specs=(hbm, hbm),
            scratch_shapes=[pltpu.SemaphoreType.DMA((2,))],
        )(*(pltpu.with_memory_space_constraint(x, pltpu.VMEM) for x in (adjoint, sens)))

    in_specs = (
        P("cond", None, "space", None, None),
        P("cond", None, "space", None, None),
        P("cond", None, None, None),
        P("cond", "space", None, None),
        P("cond"),
        P("cond"),
        P("space", None, None),
        P(None, "space"),
    )
    out_specs = (P("cond", None, "space", None, None), P("space", "cond", None))
    return jax.shard_map(local, mesh=mesh, in_specs=in_specs, out_specs=out_specs, check_vma=False)
```

```python
import functools

import jax
import jax.numpy as jnp
from jax import lax
from jax.experimental import pallas as pl
from jax.experimental.pallas import tpu as pltpu
from jax.sharding import PartitionSpec as P

RELAX = 0.7
EPS = 1.0 / 32.0
F32 = jnp.float32


def sublanes(shape):
    return lax.broadcasted_iota(jnp.int32, shape, len(shape) - 2)


def lanes(shape):
    return lax.broadcasted_iota(jnp.int32, shape, len(shape) - 1)


def up(a, n):
    return pltpu.roll(a, 8 - n, a.ndim - 2)


def down(a, n):
    return pltpu.roll(a, n, a.ndim - 2)


def ahead(a, n):
    return pltpu.roll(a, 128 - n, a.ndim - 1)


def behind(a, n):
    return pltpu.roll(a, n, a.ndim - 1)


def pack(v):
    s, z = sublanes(v[0].shape), lanes(v[0].shape)
    even, low = s % 2 == 0, s % 4 < 2
    zeven, zlow = z % 2 == 0, z % 4 < 2

    def pair(a, b):
        return jnp.where(even, a, b) + jnp.where(even, up(a, 1), down(b, 1))

    def quad(a, b):
        return jnp.where(low, a, b) + jnp.where(low, up(a, 2), down(b, 2))

    four = quad(pair(v[0], v[1]), pair(v[2], v[3]))
    last = pair(v[4], v[4])
    last = quad(last, last)
    both = jnp.where(zeven, four, last) + jnp.where(zeven, ahead(four, 1), behind(last, 1))
    return both + jnp.where(zlow, ahead(both, 2), behind(both, 2))


def unpack(c):
    s, z = sublanes(c.shape), lanes(c.shape)
    even, low, zeven = s % 2 == 0, s % 4 < 2, z % 2 == 0
    four = jnp.where(zeven, c, behind(c, 1))
    last = jnp.where(zeven, ahead(c, 1), c)
    p02 = jnp.where(even, four, down(four, 1))
    p13 = jnp.where(even, up(four, 1), four)
    return (
        jnp.where(low, p02, down(p02, 2)),
        jnp.where(low, p13, down(p13, 2)),
        jnp.where(low, up(p02, 2), p02),
        jnp.where(low, up(p13, 2), p13),
        last,
    )


def neighbours(c, first, last_box):
    own = c[1:-1]
    at = first + lax.broadcasted_iota(jnp.int32, own.shape, 0)
    z = lanes(own.shape)
    total = jnp.where(at == 0, own, c[:-2]) + jnp.where(at == last_box, own, c[2:])
    total = total + (own + up(own, 4))
    return total + jnp.where(z < 4, own, behind(own, 4)) + jnp.where(z >= 124, own, ahead(own, 4))


def coarse_solve(res, first, last_box, inverse):
    scaled = res * inverse
    c = scaled
    for sweep in range(1, 4):
        c = scaled[sweep:-sweep] + 8.0 * inverse * neighbours(c, first + sweep, last_box)
    return c


def coarse_spread(res, first, last_box, inverse):
    none = jnp.zeros((1, 8, 128), F32)
    scaled = res * inverse
    c = scaled
    for sweep in range(1, 4):
        scaled = jnp.concatenate([none, scaled, none])
        c = scaled + 8.0 * inverse * neighbours(jnp.concatenate([none, none, c, none, none]), first - sweep, last_box)
    return c


def off_diagonal(field, at, n, jac, cpx, cyz):
    s, z = sublanes((1, 8, 128)), lanes((1, 8, 128))
    y_not_last, y_not_first = jnp.where(s < 7, 1.0, 0.0), jnp.where(s >= 1, 1.0, 0.0)
    z_not_last, z_not_first = jnp.where(z < 127, 1.0, 0.0), jnp.where(z >= 1, 1.0, 0.0)
    y_far_up, y_far_down = jnp.where(s < 6, -EPS, 0.0), jnp.where(s >= 2, -EPS, 0.0)
    z_far_up, z_far_down = jnp.where(z < 126, -EPS, 0.0), jnp.where(z >= 2, -EPS, 0.0)
    cx = cpx[pl.ds(at - 2, n + 1)]
    cy_plus, cy_minus, cz_plus, cz_minus = (cyz[i, pl.ds(at - 2, n)] for i in range(4))
    center, out = [], [None] * 5

    def add(v, term):
        out[v] = term if out[v] is None else out[v] + term

    for u in range(5):
        block = field[u, pl.ds(at - 2, n + 4)]
        a, plus, minus = block[2:-2], block[3:-1], block[1:-3]
        center.append(a)
        total = cx[1:] * plus
        total = total + cx[:-1] * minus
        total = total - EPS * (block[4:] + block[:-4])
        dx = plus - minus
        plus, minus = up(a, 1), down(a, 1)
        total = total + cy_plus * plus
        total = total + cy_minus * minus
        total = total + y_far_up * up(a, 2)
        total = total + y_far_down * down(a, 2)
        dy = y_not_last * plus - y_not_first * minus
        plus, minus = ahead(a, 1), behind(a, 1)
        total = total + cz_plus * plus
        total = total + cz_minus * minus
        total = total + z_far_up * ahead(a, 2)
        total = total + z_far_down * behind(a, 2)
        dz = z_not_last * plus - z_not_first * minus
        add(u, total)
        for d, diff in enumerate((dx, dy, dz)):
            for v in range(5):
                add(v, jac[d * 25 + u * 5 + v] * diff)
    return center, out


def kernel(
    n_cond, n_space, target_in, shape_in, jac_hbm, sensor_in, shift_hbm, weight_hbm, adjoint_out, sens_out,
    jac_in, shift_in, weight_in, sen_stage, g_stage, g, sen, shp, cpx, cyz, w, diag, jac, b0, b1, b2, halo, rs, rp1, rp2, sib, cs, rc, local_sem, send_sem, recv_sem, share_sem, known_sem,
):
    space, cond = lax.axis_index("space"), lax.axis_index("cond")
    chip, core = space // 2, space % 2
    chips = n_space // 2
    has_left, has_right = chip > 0, chip < chips - 1
    has_left2, has_right2 = chip > 1, chip < chips - 2
    rows = 8 // n_cond

    ring = [(2 * chip + (core + j) % 2, lax.rem(cond + dz, n_cond)) for dz in range(n_cond) for j in range(2)]
    sibling = 2 * chip + 1 - core
    following, preceding = lax.rem(cond + 1, n_cond), lax.rem(cond + n_cond - 1, n_cond)
    beside = [(2 * (chip + near) + j, cond, there) for near, there in ((-1, has_left), (1, has_right)) for j in range(2)]
    beside += [(sibling, cond, None), (space, following, None), (space, preceding, None)]
    n_beside = 3 + 2 * (has_left.astype(jnp.int32) + has_right.astype(jnp.int32))

    def tell(semaphore, peers):
        for s, c, there in peers:
            def one(s=s, c=c):
                pl.semaphore_signal(semaphore, inc=1, device_id={"space": s, "cond": c})
            one() if there is None else pl.when(there)(one)

    barrier = pltpu.get_barrier_semaphore()
    tell(barrier, beside)

    count = iter(range(1000))
    sends = []

    def remote(src, dst, recv, s, c=cond):
        return pltpu.make_async_remote_copy(
            src_ref=src, dst_ref=dst, send_sem=send_sem.at[next(count)], recv_sem=recv_sem.at[recv],
            device_id={"space": s, "cond": c},
        )

    mine = [
        pltpu.make_async_copy(sensor_in.at[core], sen.at[pl.ds(7 + 4 * core, 4)], local_sem.at[0]),
        pltpu.make_async_copy(target_in.at[core], g.at[:, pl.ds(6 + 4 * core, 4)], local_sem.at[1]),
        pltpu.make_async_copy(shape_in.at[core], shp.at[:, pl.ds(6 + 4 * core, 4)], local_sem.at[2]),
    ]
    small = [
        pltpu.make_async_copy(jac_hbm, jac_in, local_sem.at[3]),
        pltpu.make_async_copy(shift_hbm, shift_in, local_sem.at[4]),
        pltpu.make_async_copy(weight_hbm, weight_in, local_sem.at[5]),
    ]
    stage = [
        pltpu.make_async_copy(sensor_in, sen_stage, local_sem.at[6]),
        pltpu.make_async_copy(target_in, g_stage, local_sem.at[7]),
    ]
    for copy in stage + small + mine:
        copy.start()

    pl.semaphore_wait(barrier, n_beside)
    for copy in stage:
        copy.wait()

    def to_right(k, j):
        low, size, at = ((2, 2, 0), (0, 4, 2))[k]
        s_low, s_size, s_at = ((1, 3, 0), (0, 4, 3))[k]
        there = 2 * (chip + 1) + j
        return [
            remote(sen_stage.at[j, pl.ds(s_low, s_size)], sen.at[pl.ds(s_at, s_size)], 3 + 2 * k, there),
            remote(g_stage.at[j, :, pl.ds(low, size)], g.at[:, pl.ds(at, size)], 4 + 2 * k, there),
            remote(shape_in.at[j, :, pl.ds(low, size)], shp.at[:, pl.ds(at, size)], 21 + k, there),
        ]

    def to_left(k, j):
        size, at = ((4, 14), (2, 18))[k]
        s_size, s_at = ((4, 15), (3, 19))[k]
        there = 2 * (chip - 1) + j
        return [
            remote(sen_stage.at[j, pl.ds(0, s_size)], sen.at[pl.ds(s_at, s_size)], 7 + 2 * k, there),
            remote(g_stage.at[j, :, pl.ds(0, size)], g.at[:, pl.ds(at, size)], 8 + 2 * k, there),
            remote(shape_in.at[j, :, pl.ds(0, size)], shp.at[:, pl.ds(at, size)], 23 + k, there),
        ]

    first_round = []
    for near in (True, False):
        for make, there, k in ((to_right, has_right, 1 if near else 0), (to_left, has_left, 0 if near else 1)):
            pairs = [make(k, j) for j in range(2)]
            first_round.append(([[c[i] for c in pairs] for i in range(3)], jnp.logical_and(there, core == k)))
    other = 1 - core
    swap = [
        remote(sen_stage.at[other], sen.at[pl.ds(7 + 4 * core, 4)], 0, sibling),
        remote(g_stage.at[other], g.at[:, pl.ds(6 + 4 * core, 4)], 1, sibling),
        remote(shape_in.at[other], shp.at[:, pl.ds(6 + 4 * core, 4)], 2, sibling),
    ]
    def send_first(items):
        for copies, there in items:
            @pl.when(there)
            def _(copies=copies):
                for copy in copies[0] + copies[1]:
                    copy.start()

    send_first(first_round[:2])
    for copy in swap[:2]:
        copy.start()
    send_first(first_round[2:])
    swap[2].start()
    for copies, there in first_round:
        @pl.when(there)
        def _(copies=copies):
            for copy in copies[2]:
                copy.start()

    tell(known_sem.at[0], beside)

    @pl.when(jnp.logical_not(has_left))
    def _():
        g[:, 0:6] = jnp.zeros((5, 6, 8, 128), F32)
        sen[0:7] = jnp.zeros((7, 8, 128), F32)
        halo[:, 0:6] = jnp.zeros((5, 6, 8, 128), F32)
        rp1[3:7] = jnp.zeros((4, 8, 128), F32)
        rp2[:, 0:3] = jnp.zeros((2, 3, 8, 128), F32)
        rc[0] = jnp.zeros(rc.shape[1:], F32)

    @pl.when(jnp.logical_not(has_right))
    def _():
        g[:, 14:20] = jnp.zeros((5, 6, 8, 128), F32)
        sen[15:22] = jnp.zeros((7, 8, 128), F32)
        halo[:, 6:12] = jnp.zeros((5, 6, 8, 128), F32)
        rp1[11:15] = jnp.zeros((4, 8, 128), F32)
        rp2[:, 7:10] = jnp.zeros((2, 3, 8, 128), F32)
        rc[2] = jnp.zeros(rc.shape[1:], F32)

    @pl.when(jnp.logical_not(has_left2))
    def _():
        rp1[0:3] = jnp.zeros((3, 8, 128), F32)

    @pl.when(jnp.logical_not(has_right2))
    def _():
        rp1[15:18] = jnp.zeros((3, 8, 128), F32)

    for copy in small:
        copy.wait()
    for d in range(3):
        for u in range(5):
            for v in range(5):
                jac[d * 25 + u * 5 + v] = jnp.full((8, 128), 0.5 * jac_in[d, u, core, v], F32)
    shift = jnp.full((8, 128), shift_in[core], F32)
    inverse = 1.0 / (shift * 32.0 + 48.0)

    from_left, from_right = ([make(k, 0) for k in range(2)] for make in (to_right, to_left))

    def arrive_first(i, copies, there):
        @pl.when(there)
        def _():
            for copy in copies:
                copy[i].wait_recv()

    mine[0].wait()
    swap[0].wait_recv()
    arrive_first(0, from_left, has_left)

    s, z = sublanes((1, 8, 128)), lanes((1, 8, 128))

    def coefficients(k, carry):
        i = 4 * k
        block = sen[pl.ds(i, 6)]
        near = block[1:5]
        x_plus, x_minus = (near + block[2:]) * 0.25, (near + block[:4]) * 0.25
        y_plus = (near + jnp.where(s < 7, up(near, 1), 0.0)) * 0.25
        y_minus = (near + jnp.where(s >= 1, down(near, 1), 0.0)) * 0.25
        z_plus = (near + jnp.where(z < 127, ahead(near, 1), 0.0)) * 0.25
        z_minus = (near + jnp.where(z >= 1, behind(near, 1), 0.0)) * 0.25
        total = shift[None] + ((x_plus + x_minus) + (y_plus + y_minus) + (z_plus + z_minus)) + 18.0 * EPS
        cpx[pl.ds(i + 1, 4)] = x_plus + 4.0 * EPS
        cyz[0, pl.ds(i, 4)] = jnp.where(s < 7, y_plus + 4.0 * EPS, 0.0)
        cyz[1, pl.ds(i, 4)] = jnp.where(s >= 1, y_minus + 4.0 * EPS, 0.0)
        cyz[2, pl.ds(i, 4)] = jnp.where(z < 127, z_plus + 4.0 * EPS, 0.0)
        cyz[3, pl.ds(i, 4)] = jnp.where(z >= 1, z_minus + 4.0 * EPS, 0.0)
        at = i + lax.broadcasted_iota(jnp.int32, total.shape, 0)
        inside = jnp.logical_and(at >= low_layer, at < high_layer)
        diag[pl.ds(i, 4)] = total
        w[pl.ds(i, 4)] = jnp.where(inside, RELAX / total, 0.0)
        return carry

    low_layer, high_layer = jnp.where(has_left, 0, 6), jnp.where(has_right, 20, 14)
    cpx[0:1] = (sen[0:1] + sen[1:2]) * 0.25 + 4.0 * EPS
    lax.fori_loop(0, 3, coefficients, 0)

    right, left = space + 2, space - 2

    def start(copies):
        for copy, there in copies:
            pl.when(there)(copy.start)

    def arrive(copies, theres):
        for (copy, _), there in zip(copies, theres):
            pl.when(there)(copy.wait_recv)

    def sent(copies):
        for copy, there in copies:
            pl.when(there)(copy.wait_send)

    def begin(k, carry):
        i = 4 * k
        weight = w[pl.ds(i, 4)]
        for v in range(5):
            b0[v, pl.ds(i + 2, 4)] = weight * g[v, pl.ds(i, 4)]
        return carry

    def sweep(src, dst, low, n, times, stride=None):
        part = 2

        def body(i, carry):
            results = []
            for k in range(n // part):
                at = low + i * (stride or n) + k * part
                center, out = off_diagonal(src, at, part, jac, cpx, cyz)
                weight = w[pl.ds(at - 2, part)]
                results.append([
                    (1.0 - RELAX) * center[v] + weight * (g[v, pl.ds(at - 2, part)] + out[v]) for v in range(5)
                ])
            for k, values in enumerate(results):
                for v in range(5):
                    dst[v, pl.ds(low + i * (stride or n) + k * part, part)] = values[v]
            return carry

        lax.fori_loop(0, times, body, 0)

    def restrict(src):
        def body(i, carry):
            at = 8 + i * 4
            center, out = off_diagonal(src, at, 4, jac, cpx, cyz)
            d = diag[pl.ds(at - 2, 4)]
            for v in range(5):
                r = g[v, pl.ds(at - 2, 4)] + out[v] - d * center[v]
                rs[v, pl.ds(2 * i, 1)] = r[0:1] + r[1:2]
                rs[v, pl.ds(2 * i + 1, 1)] = r[2:3] + r[3:4]
            return carry

        lax.fori_loop(0, 2, body, 0)
        return pack([rs[v] for v in range(5)])

    mine[1].wait()
    swap[1].wait_recv()
    arrive_first(1, from_left, has_left)
    lax.fori_loop(0, 3, begin, 0)
    sweep(b0, b1, 4, 8, 1)
    sweep(b1, b2, 6, 4, 1)
    early_halo = [(remote(b2.at[:, pl.ds(8, 2)], halo.at[:, pl.ds(0, 2)], 29, right), has_right)]
    start(early_halo)
    arrive_first(0, from_right, has_right)
    lax.fori_loop(3, 5, coefficients, 0)
    arrive_first(1, from_right, has_right)
    lax.fori_loop(3, 5, begin, 0)
    sweep(b0, b1, 12, 8, 1)
    sweep(b1, b2, 10, 8, 1)
    pl.semaphore_wait(known_sem.at[0], n_beside)
    tell(known_sem.at[1], [(space, preceding, None)])
    near_halos = [
        (remote(b2.at[:, pl.ds(12, 2)], halo.at[:, pl.ds(4, 2)], 11, right), has_right),
        (remote(b2.at[:, pl.ds(10, 2)], halo.at[:, pl.ds(6, 2)], 12, left), has_left),
    ]
    far_halos = [
        (remote(b2.at[:, pl.ds(10, 2)], halo.at[:, pl.ds(2, 2)], 19, right), has_right),
        (remote(b2.at[:, pl.ds(12, 4)], halo.at[:, pl.ds(8, 4)], 20, left), has_left),
    ]
    start(near_halos)
    rp1[7:11] = restrict(b2)
    boxes = [
        (remote(rp1.at[pl.ds(7, 4)], rp1.at[pl.ds(3, 4)], 15, right), has_right),
        (remote(rp1.at[pl.ds(7, 4)], rp1.at[pl.ds(11, 4)], 16, left), has_left),
        (remote(rp1.at[pl.ds(8, 3)], rp1.at[pl.ds(0, 3)], 13, space + 4), has_right2),
        (remote(rp1.at[pl.ds(7, 3)], rp1.at[pl.ds(15, 3)], 14, space - 4), has_left2),
    ]
    start(boxes)
    start(far_halos)
    arrive(boxes, (has_left, has_right, has_left2, has_right2))
    last_box = 4 * chips - 1
    c = coarse_solve(rp1[...], 4 * chip - 7, last_box, inverse[None])
    at = 4 * chip - 4 + lax.broadcasted_iota(jnp.int32, c.shape, 0)
    fixes = unpack(jnp.where(jnp.logical_and(at >= 0, at <= last_box), c, 0.0))

    def correct(old, low, high):
        for v in range(5):
            for i in range(low, high):
                b1[v, i] = old(v, i) + fixes[v][i // 2]

    arrive(near_halos, (has_left, has_right))
    correct(lambda v, i: halo[v, i], 4, 6)
    correct(lambda v, i: b2[v, i], 6, 18)
    correct(lambda v, i: halo[v, i - 12], 18, 20)
    sweep(b1, b0, 6, 6, 2)
    sweep(b0, b1, 8, 8, 1)
    arrive(early_halo + far_halos, (has_left, has_left, has_right))
    correct(lambda v, i: halo[v, i], 0, 4)
    correct(lambda v, i: halo[v, i - 12], 20, 24)
    sweep(b1, b0, 2, 4, 2, 16)
    sweep(b0, b1, 4, 4, 2, 12)
    sweep(b1, b0, 6, 6, 2)
    over = remote(b0.at[:, pl.ds(8 + 4 * other, 4)], sib, 25, sibling)
    over.start()
    rp2[core, 3:7] = restrict(b0)

    def boxes_beside(c_at, j):
        return [
            (remote(rp2.at[c_at, pl.ds(4, 3)], rp2.at[c_at, pl.ds(0, 3)], 17 + 9 * c_at, right - core + j), has_right),
            (remote(rp2.at[c_at, pl.ds(3, 3)], rp2.at[c_at, pl.ds(7, 3)], 18 + 9 * c_at, left - core + j), has_left),
        ]

    boxes2 = boxes_beside(core, 0) + boxes_beside(core, 1)

    weight = jnp.full((8, 128), weight_in[core], F32)
    mine[2].wait()
    swap[2].wait_recv()
    arrive_first(2, from_left, has_left)
    arrive_first(2, from_right, has_right)
    fixes = unpack(coarse_spread(rp2[core, 3:7], 4 * chip, last_box, inverse[None]))
    parts = []
    for i in range(20):
        total = None
        for v in range(5):
            value = fixes[v][i // 2]
            if 6 <= i < 14:
                value = value + b0[v, 2 + i]
            term = value * shp[v, i]
            total = term if total is None else total + term
        parts.append(weight * total)
    me = 2 * cond + core

    def share(d, j, c_to):
        return pltpu.make_async_remote_copy(
            src_ref=cs.at[d, j * n_cond + c_to], dst_ref=rc.at[2 - d, me], send_sem=share_sem.at[d], recv_sem=share_sem.at[5 - d],
            device_id={"space": 2 * (chip + d - 1) + j, "cond": c_to},
        )

    def shared(d, slots):
        return pltpu.make_async_remote_copy(
            src_ref=cs.at[d, pl.ds(0, slots)], dst_ref=rc.at[d, pl.ds(0, slots)], send_sem=share_sem.at[d], recv_sem=share_sem.at[3 + d],
            device_id={"space": sibling, "cond": cond},
        )

    pl.semaphore_wait(known_sem.at[1], 1)
    s2 = sublanes((8, 128))

    def gather(d):
        for j in range(2):
            for c_to in range(n_cond):
                gathered = jnp.zeros((8, 128), F32)
                for i in range(4):
                    at = 8 * d - 2 + 4 * j + i
                    turn = (rows * i - rows * c_to) % 8
                    moved = jnp.zeros((8, 128), F32)
                    if 0 <= at < 20:
                        moved = parts[at] if turn == 0 else down(parts[at], turn)
                    gathered = jnp.where(s2 >= rows * i, moved, gathered) if i else moved
                cs[d, j * n_cond + c_to] = gathered

    outer = ((0, has_left), (2, has_right))
    gather(0)
    gather(2)
    for dz in (2, 1, 3, 0):
        for d, there in outer:
            @pl.when(there)
            def _(d=d, dz=dz):
                for j in range(2):
                    share(d, j, lax.rem(cond + dz, n_cond)).start()
    gather(1)
    for s_to, c_to in reversed(ring[1:]):
        share(1, lax.rem(s_to, 2), c_to).start()
    rc[1, me] = cs[1, core * n_cond + cond]

    start(boxes2)
    boxes_over = remote(rp2.at[core, pl.ds(3, 4)], rp2.at[core, pl.ds(3, 4)], 28, sibling)
    boxes_over.start()

    arrive(boxes_beside(0, 0) + boxes_beside(1, 0), (has_left, has_right) * 2)
    boxes_over.wait_recv()
    over.wait_recv()
    for c_at, old in ((core, lambda v: b0[v, pl.ds(8 + 4 * core, 4)]), (other, lambda v: sib[v])):
        inv = 1.0 / (jnp.full((1, 8, 128), shift_in[c_at], F32) * 32.0 + 48.0)
        c = coarse_solve(rp2[c_at, pl.ds(2 * core, 8)], 4 * chip - 3 + 2 * core, last_box, inv)
        fixes = unpack(c)
        for v in range(5):
            value = old(v)
            for i in range(4):
                adjoint_out[c_at, v, i] = value[i] + fixes[v][i // 2]

    over.wait_send()
    boxes_over.wait_send()
    for copy in swap:
        copy.wait_send()
    for copies, there in first_round:
        @pl.when(there)
        def _(copies=copies):
            for copy in copies[0] + copies[1] + copies[2]:
                copy.wait_send()
    sent(early_halo + near_halos + far_halos + boxes + boxes2)

    def group(d):
        pairs = [rc[d, i] + rc[d, i + n_cond] for i in range(n_cond)]
        return sum(pairs[1:], pairs[0])

    shared(1, 2 * n_cond - 1).wait_recv()
    total = group(1)
    for d, there in outer:
        pl.when(there)(shared(d, 2 * n_cond).wait_recv)
    total = total + (group(0) + group(2))
    for i in range(4):
        sens_out[i] = total[rows * i : rows * (i + 1)]
    for d, there in outer:
        pl.when(there)(shared(d, 2 * n_cond).wait_send)
    shared(1, 2 * n_cond - 1).wait_send()


def settle(adjoint, sens, adjoint_out, sens_out, sem):
    copies = [pltpu.make_async_copy(adjoint, adjoint_out, sem.at[0]), pltpu.make_async_copy(sens, sens_out, sem.at[1])]
    for copy in copies:
        copy.start()
    for copy in copies:
        copy.wait()


def solution(mesh):
    n_cond, n_space = mesh.shape["cond"], mesh.shape["space"]
    rows = 8 // n_cond

    def local(target, shape, jac, sensor, shift, weight, agglomeration, links):
        vmem = lambda *shape: pltpu.VMEM((*shape, 8, 128), F32)
        hbm = pl.BlockSpec(memory_space=pltpu.HBM)
        stay = lambda x: pltpu.with_memory_space_constraint(x, pltpu.HBM)
        operands = (target, shape, jnp.transpose(jac, (1, 2, 0, 3)), sensor, shift, weight)
        adjoint, sens = pl.pallas_call(
            functools.partial(kernel, n_cond, n_space),
            out_shape=(
                pltpu.VMEM(target.shape, F32),
                pltpu.VMEM((4, rows, 128), F32),
            ),
            in_specs=[hbm] * 6,
            out_specs=(pl.BlockSpec(memory_space=pltpu.VMEM),) * 2,
            scratch_shapes=[
                pltpu.SMEM((3, 5, 2, 5), F32), pltpu.SMEM((2,), F32), pltpu.SMEM((2,), F32),
                vmem(2, 4), vmem(2, 5, 4),
                vmem(5, 20), vmem(22), vmem(5, 20),
                vmem(21), vmem(4, 20), vmem(20), vmem(20), vmem(75),
                vmem(5, 24), vmem(5, 24), vmem(5, 24), vmem(5, 12), vmem(5, 4),
                vmem(18), vmem(2, 10), vmem(5, 4), vmem(3, 2 * n_cond), vmem(3, 2 * n_cond),
                pltpu.SemaphoreType.DMA((8,)),
                pltpu.SemaphoreType.DMA((64,)),
                pltpu.SemaphoreType.DMA((30,)),
                pltpu.SemaphoreType.DMA((6,)),
                pltpu.SemaphoreType.REGULAR((2,)),
            ],
            compiler_params=pltpu.CompilerParams(
                collective_id=0, has_side_effects=True, vmem_limit_bytes=48 * 2**20
            ),
        )(*map(stay, operands))
        return pl.pallas_call(
            settle,
            out_shape=(pltpu.HBM(adjoint.shape, F32), pltpu.HBM(sens.shape, F32)),
            in_specs=[pl.BlockSpec(memory_space=pltpu.VMEM)] * 2,
            out_specs=(hbm, hbm),
            scratch_shapes=[pltpu.SemaphoreType.DMA((2,))],
        )(*(pltpu.with_memory_space_constraint(x, pltpu.VMEM) for x in (adjoint, sens)))

    in_specs = (
        P("cond", None, "space", None, None),
        P("cond", None, "space", None, None),
        P("cond", None, None, None),
        P("cond", "space", None, None),
        P("cond"),
        P("cond"),
        P("space", None, None),
        P(None, "space"),
    )
    out_specs = (P("cond", None, "space", None, None), P("space", "cond", None))
    return jax.shard_map(local, mesh=mesh, in_specs=in_specs, out_specs=out_specs, check_vma=False)
```
